512 devices in a mesh: leaf: 128 (over y, z, core), probe: 4 (over x).
Axes of the slice: x: 4, y: 8, z: 8, core: 2. Of those that a mesh axis runs over, the one named last changes fastest.
Arguments:
- points: bfloat16 [262144, 64], P('leaf'), may hold values from -6 to 6
- probes: bfloat16 [262144, 256], P('leaf', 'probe'), may hold values from -6 to 6
- near_list: int32 [1024, 16], P('leaf'), may hold values from 0 to 1023, as said below
- near_count: int32 [1024], P('leaf'), may hold values from 1 to 16, as said below
Outputs:
- samples: float32 [262144, 256], P('leaf', 'probe')
- node_factors: float32 [128, 3, 256, 256], P('leaf')
- root_factor: float32 [256, 256], replicated
The draws below stay inside these ranges and needn't reach their ends.
Inputs may be any that keep to these rules, and one draw needn't show every extreme that they name: near_list[i, 0] = i; every id lies within 8 boxes of i. `near_count`: the first box of each device has all 16 slots live.
All inputs are finite; a program needn't handle non-finite values.
Results may differ from the reference program's by a relative error of at most 0.0003.
Values may be sent and summed in bfloat16 or wider, within the bound.
No kernel may reach another device: no remote copies, remote signals or barrier semaphores. Data moves between devices by JAX's collectives and lax.ppermute only.
A program may use at most 64 MiB of HBM per device.

```python
import jax
import jax.numpy as jnp
from jax import lax

BOX = 256
DF = 64
RK = 256
NEAR = 16
LEVELS = 3
BLK_DEV = 8
NBLK = 1024
NPTS = 262144
N_LEAF = 128


def draw_near_list(key, part):
    key = jax.random.fold_in(key, 11)
    shifts = jax.random.randint(key, (NBLK, NEAR), -BLK_DEV, BLK_DEV + 1)
    rows = jnp.arange(NBLK, dtype=jnp.int32)[:, None]
    ids = jnp.clip(rows + shifts, 0, NBLK - 1)
    return ids.at[:, 0].set(rows[:, 0]).astype(jnp.int32)


def draw_near_count(key, part):
    key = jax.random.fold_in(key, 23)
    counts = jax.random.randint(key, (NBLK,), 1, NEAR + 1)
    first = jnp.arange(NBLK, dtype=jnp.int32) % BLK_DEV == 0
    return jnp.where(first, NEAR, counts).astype(jnp.int32)


def levels(own_key, shape, pieces, smallest, high):
    def one(position, shards_of):
        draws = jax.random.uniform(jax.random.fold_in(jax.random.fold_in(own_key, 6), position), (shards_of,), jnp.float32, smallest / len(pieces), high / len(pieces))
        return jnp.repeat(jnp.exp(draws), shape[position] // shards_of).reshape((-1,) + (1,) * (len(shape) - position - 1))

    loudness = one(*pieces[0])
    for cut in pieces[1:]:
        loudness = loudness * one(*cut)
    return loudness


def noise(stream_key, shape, scale, most, pieces=(), kind=jnp.bfloat16):
    array = scale * jax.random.normal(stream_key, shape, jnp.float32)
    if pieces:
        array = array * levels(stream_key, shape, pieces, -0.22, 0.18)
    return jnp.clip(array, -most, most).astype(kind)


def setup_inputs(seed: int = 0) -> dict:
    key_of = jax.random.split(jax.random.key(seed), 5)
    return {
        "points": noise(key_of[0], (NPTS, DF), 1.0, 6.0, ((0, 128),)),
        "probes": noise(key_of[1], (NPTS, RK), 1.0, 6.0, ((0, 128), (1, 4))),
        "near_list": draw_near_list(jax.random.fold_in(key_of[4], 71), 0),
        "near_count": draw_near_count(jax.random.fold_in(key_of[4], 71), 0),
    }


def group_samples(points_g, probes_g, ids_g, counts_g, boxes_x, boxes_o):
    own = points_g.astype(jnp.float32)
    sq_own = jnp.sum(own * own, axis=-1)
    total = jnp.zeros((BLK_DEV, BOX, RK), jnp.float32)
    for slot in range(NEAR):
        index = ids_g[:, slot]
        other = boxes_x[index].astype(jnp.float32)
        sq_other = jnp.sum(other * other, axis=-1)
        cross = jnp.einsum('bid,bjd->bij', own, other, precision=lax.Precision.HIGHEST)
        dist = sq_own[:, :, None] + sq_other[:, None, :] - 2.0 * cross
        live = (slot < counts_g).astype(jnp.float32)
        tile = jnp.exp(-dist / (DF / 2.0)) * live[:, None, None]
        total = total + jnp.einsum('bij,bjr->bir', tile, boxes_o[index].astype(jnp.float32), precision=lax.Precision.HIGHEST)
    return total

def reference(points, probes, near_list, near_count):
    boxes_x = points.reshape(NBLK, BOX, DF)
    boxes_o = probes.reshape(NBLK, BOX, RK)

    def per_group(g):
        start = g * BLK_DEV
        return group_samples(lax.dynamic_slice_in_dim(boxes_x, start, BLK_DEV, 0), lax.dynamic_slice_in_dim(boxes_o, start, BLK_DEV, 0), lax.dynamic_slice_in_dim(near_list, start, BLK_DEV, 0), lax.dynamic_slice_in_dim(near_count, start, BLK_DEV, 0), boxes_x, boxes_o)
    samples = lax.map(per_group, jnp.arange(N_LEAF, dtype=jnp.int32)).reshape(NPTS, RK)
    grouped = samples.reshape(N_LEAF, BLK_DEV * BOX, RK)
    grams = jnp.einsum('gnr,gns->grs', grouped, grouped, precision=lax.Precision.HIGHEST)
    eye = jnp.eye(RK, dtype=jnp.float32)
    factors = []
    for level in range(1, LEVELS + 1):
        width = 2 ** level
        sums = grams.reshape(N_LEAF // width, width, RK, RK).sum(axis=1)
        chol = jnp.linalg.cholesky(sums / (BLK_DEV * BOX * width) + eye)
        factors.append(jnp.repeat(chol, width, axis=0))
    node_factors = jnp.stack(factors, axis=1)
    root_factor = jnp.linalg.cholesky(jnp.sum(grams, axis=0) / NPTS + eye)
    return (samples, node_factors, root_factor)
```

```python
import functools

import jax
import jax.numpy as jnp
from jax import lax
from jax.experimental import pallas as pl
from jax.experimental.pallas import tpu as pltpu
from jax.sharding import Mesh, PartitionSpec as P

LEVELS = 3
BLOCKS = 8
BOX = 256
SLOTS = 16
STEPS = BLOCKS * SLOTS // 2 + 16
BF = jnp.bfloat16
F = jnp.float32
NN = (((1,), (0,)), ((), ()))
NT = (((1,), (1,)), ((), ()))
TN = (((0,), (0,)), ((), ()))
LOG2E_OVER_32 = 1.4426950408889634 / 32.0
LIMIT = 48 << 20
VM = pl.BlockSpec(memory_space=pltpu.VMEM)
SM = pl.BlockSpec(memory_space=pltpu.SMEM)


def dot(a, b, dims):
    return lax.dot_general(a, b, dims, preferred_element_type=F)


def squares(x):
    wide = x.astype(F)
    wide = wide * wide
    high = wide.astype(BF)
    return high, (wide - high.astype(F)).astype(BF)


def split3(x):
    h = x.astype(BF)
    r = x - h.astype(F)
    m = r.astype(BF)
    return h, m, (r - m.astype(F)).astype(BF)


def list_steps(offsets, base, list_ref, count_ref, ids):
    for e in range(2):
        for r in range(3):
            ids[r, e] = 0
        ids[3, e] = 1
        ids[4, e] = 1

    def box_list(b, n):
        def one(s, carry):
            n, half = carry
            j = list_ref[b, s] - base
            hit = None
            place = jnp.int32(0)
            for q, off in enumerate(offsets):
                inside = jnp.logical_and(j >= off, j < off + BLOCKS)
                place = jnp.where(inside, j - off + BLOCKS * q, place)
                hit = inside if hit is None else jnp.logical_or(hit, inside)

            @pl.when(jnp.logical_and(hit, half == 0))
            def _():
                ids[0, n] = b
                ids[1, n] = place
                ids[2, n] = place
                ids[3, n] = 0
                ids[4, n] = 1

            @pl.when(jnp.logical_and(hit, half == 1))
            def _():
                ids[2, n - 1] = place
                ids[4, n - 1] = 0

            h = hit.astype(jnp.int32)
            return n + jnp.where(half == 0, h, 0), half ^ h

        n, _ = lax.fori_loop(0, count_ref[b], one, (n, jnp.int32(0)))
        return n

    n = lax.fori_loop(0, BLOCKS, box_list, jnp.int32(2))
    for e in range(2):
        for r in range(3):
            ids[r, n + e] = 0
        ids[3, n + e] = 1
        ids[4, n + e] = 1
    return n


def tiles_kernel(offsets, first, base_ref, list_ref, count_ref, own_ref, *rest):
    count = len(offsets)
    source_refs, rest = rest[:count], rest[count:]
    if first:
        total = rest[0]
        rest = rest[1:]
    else:
        previous, samples_ref, send_ref = rest[:3]
        total = rest[-1]
        rest = rest[3:-1]
    sq_own, sq_other, left, boxes, ids, cross, parts = rest
    points_lane = lax.broadcasted_iota(jnp.int32, (BOX, 128), 1) >= 64
    ones_row = jnp.where(lax.broadcasted_iota(jnp.int32, (8, 128), 1) >= 64, 1.0, 0.0).astype(BF)
    ones_all = jnp.where(lax.broadcasted_iota(jnp.int32, (128, 128), 0) >= 64, 1.0, 0.0).astype(BF)
    n = list_steps(offsets, base_ref[0], list_ref, count_ref, ids)
    for b in range(BLOCKS):
        x = own_ref[b]
        h, l = squares(x)
        sq_own[b] = dot(h, ones_all, NN) + dot(l, ones_all, NN)
        left[b] = jnp.where(points_lane, x.astype(F) * 2.0, 0.0).astype(BF)
        total[b] = jnp.zeros((BOX, 128), F) if first else previous[b]
    for q in range(count):
        for b in range(BLOCKS):
            x = source_refs[q][b]
            boxes[BLOCKS * q + b] = x
            h, l = squares(x)
            sq_other[BLOCKS * q + b] = dot(ones_row, h, NT) + dot(ones_row, l, NT)
    cross[...] = jnp.zeros_like(cross)
    parts[...] = jnp.zeros_like(parts)

    def entry(t):
        return tuple(ids[r, t] for r in range(5))

    def step(t, _):
        i, a, b, _, _ = entry(t - 2)
        columns = jnp.concatenate([boxes[a], boxes[b], boxes[a], boxes[b]], axis=0)
        total[i] = total[i] + dot(parts[...], columns, NN)
        i, a, b, dead_a, dead_b = entry(t - 1)
        own_sq = sq_own[i]
        own_sq = jnp.concatenate([own_sq, own_sq], axis=1)
        x = cross[...]
        high, low = [], []
        for c, (slot, dead) in enumerate(((a, dead_a), (b, dead_b))):
            row = sq_other[slot][0:1, :] + dead.astype(F) * 1e30
            tile = jnp.exp2((x[:, BOX * c:BOX * c + BOX] - row - own_sq) * LOG2E_OVER_32)
            h = tile.astype(BF)
            high.append(h)
            low.append((tile - h.astype(F)).astype(BF))
        parts[...] = jnp.concatenate(high + low, axis=1)
        i, a, b, _, _ = entry(t)
        cross[...] = dot(left[i], jnp.concatenate([boxes[a], boxes[b]], axis=0), NT)
        return 0

    lax.fori_loop(2, n + 2, step, 0)
    if not first:
        for b in range(BLOCKS):
            samples_ref[BOX * b:BOX * b + BOX, :] = total[b][:, :64]
        for p in range(BLOCKS // 2):
            send_ref[p] = jnp.concatenate([total[2 * p][:, :64], total[2 * p + 1][:, :64]], axis=1)


def tiles(base, near_list, near_count, own, sources, offsets, previous=None):
    first = previous is None
    count = len(sources)
    args = [base, near_list, near_count, own] + list(sources)
    totals = jax.ShapeDtypeStruct((BLOCKS, BOX, 128), F)
    if first:
        out_shape, out_specs = totals, VM
    else:
        args.append(previous)
        out_shape = (
            jax.ShapeDtypeStruct((BLOCKS * BOX, 64), F),
            jax.ShapeDtypeStruct((BLOCKS // 2, BOX, 128), F),
        )
        out_specs = (VM, VM)
    scratch = [
        pltpu.VMEM((BLOCKS, BOX, 128), F),
        pltpu.VMEM((BLOCKS * count, 8, BOX), F),
        pltpu.VMEM((BLOCKS, BOX, 128), BF),
        pltpu.VMEM((BLOCKS * count, BOX, 128), BF),
        pltpu.SMEM((5, STEPS), jnp.int32),
        pltpu.VMEM((BOX, 2 * BOX), F),
        pltpu.VMEM((BOX, 4 * BOX), BF),
    ]
    if not first:
        scratch.append(pltpu.VMEM((BLOCKS, BOX, 128), F))
    return pl.pallas_call(
        functools.partial(tiles_kernel, offsets, first),
        out_shape=out_shape,
        in_specs=[SM] * 3 + [VM] * (len(args) - 3),
        out_specs=out_specs,
        scratch_shapes=scratch,
        compiler_params=pltpu.CompilerParams(vmem_limit_bytes=LIMIT),
        cost_estimate=pl.CostEstimate(
            flops=60 * 4 * BOX * BOX * 128 * 2, bytes_accessed=4 << 20, transcendentals=60 * BOX * BOX
        ),
    )(*args)


def gram_kernel(columns_ref, out_ref):
    s = jnp.concatenate(
        [
            jnp.concatenate([columns_ref[q][:, 64 * h:64 * h + 64] for q in range(4)], axis=1)
            for h in range(2)
        ],
        axis=0,
    )
    h, m, l = split3(s)
    left = jnp.concatenate([h, h, m, h, m, l], axis=0)
    right = jnp.concatenate([h, m, h, l, m, h], axis=0)
    g = dot(left, right, TN)
    out_ref[0:128, :] = g[0:128, 0:128]
    out_ref[128:256, :] = g[0:128, 128:256]
    out_ref[256:384, :] = g[128:256, 128:256]


def gram(columns):
    return pl.pallas_call(
        gram_kernel,
        out_shape=jax.ShapeDtypeStruct((384, 128), F),
        in_specs=[VM],
        out_specs=VM,
        compiler_params=pltpu.CompilerParams(vmem_limit_bytes=LIMIT),
    )(columns)


def panel_step(rows, off, width):
    n = len(rows)
    lanes = range(width // 128)
    sub = lax.broadcasted_iota(jnp.int32, (8, 128), 0)
    part = [[[r[8 * g:8 * g + 8, 128 * q:128 * q + 128] for q in lanes] for g in range(4)] for r in rows]
    for s in range(4):
        at = off + 8 * s
        cols = [
            [
                None if g < s else [
                    jnp.broadcast_to(part[b][g][0][:, at + j:at + j + 1], (8, 128)) for j in range(8)
                ]
                for g in range(4)
            ]
            for b in range(n)
        ]
        scale = [None] * n
        for j in range(8):
            for b in range(n):
                here = cols[b][s]
                pivot = jnp.broadcast_to(here[j][j:j + 1, :], (8, 128))
                inverse = 1.0 / pivot
                root = lax.rsqrt(pivot)
                scale[b] = root if j == 0 else jnp.where(sub == j, root, scale[b])
                ratio = [
                    None if l <= j else jnp.broadcast_to(here[l][j:j + 1, :], (8, 128)) * inverse
                    for l in range(8)
                ]
                row = [jnp.broadcast_to(part[b][s][q][j:j + 1, :], (8, 128)) * inverse for q in lanes]
                for g in range(s, 4):
                    c = cols[b][g][j]
                    for l in range(j + 1, 8):
                        cols[b][g][l] = cols[b][g][l] - c * ratio[l]
                    if g == s:
                        c = jnp.where(sub > j, c, 0.0)
                    part[b][g] = [part[b][g][q] - c * row[q] for q in lanes]
        for b in range(n):
            part[b][s] = [v * scale[b] for v in part[b][s]]
    return [jnp.concatenate([jnp.concatenate(v, axis=1) for v in p], axis=0) for p in part]


def factor(n, work, upper):
    for half in range(2):
        c0 = 128 * half
        for k in range(4):
            r0 = c0 + 32 * k
            rows = panel_step([work[b, r0:r0 + 32, c0:256] for b in range(n)], 32 * k, 256 - c0)
            for b in range(n):
                upper[b, r0:r0 + 32, c0:256] = rows[b]
            lo = r0 + 32
            if lo == 256:
                break
            for b in range(n):
                h, m, l = split3(rows[b])
                left = jnp.concatenate([h, h, m, h, m, l], axis=0)
                right = jnp.concatenate([h, m, h, l, m, h], axis=0)
                work[b, lo:256, c0:256] = work[b, lo:256, c0:256] - dot(left, right, TN)[lo - c0:, :]


def factor_kernel(scales, slices_ref, nodes_ref, root_ref, work, upper):
    n = len(scales)
    ri = lax.broadcasted_iota(jnp.int32, (128, 128), 0)
    ci = lax.broadcasted_iota(jnp.int32, (128, 128), 1)
    eye = jnp.where(ri == ci, 1.0, 0.0)
    for b in range(n):
        tri = jnp.concatenate([slices_ref[r, b] for r in range(8)], axis=0) * scales[b]
        work[b, 0:128, 0:128] = tri[0:128] + eye
        work[b, 0:128, 128:256] = tri[128:256]
        work[b, 128:256, 0:128] = jnp.zeros((128, 128), F)
        work[b, 128:256, 128:256] = tri[256:384] + eye
        upper[b, 128:256, 0:128] = jnp.zeros((128, 128), F)
    factor(n, work, upper)
    rows = lax.broadcasted_iota(jnp.int32, (256, 256), 0)
    cols = lax.broadcasted_iota(jnp.int32, (256, 256), 1)
    for b in range(n):
        low = jnp.where(rows >= cols, upper[b].T, 0.0)
        if b < LEVELS:
            nodes_ref[0, b] = low
        else:
            root_ref[...] = low


def factors(slices, scales):
    n = len(scales)
    return pl.pallas_call(
        functools.partial(factor_kernel, scales),
        out_shape=(
            jax.ShapeDtypeStruct((1, LEVELS, 256, 256), F),
            jax.ShapeDtypeStruct((256, 256), F),
        ),
        in_specs=[VM],
        out_specs=(VM, VM),
        scratch_shapes=[pltpu.VMEM((n, 256, 256), F)] * 2,
        compiler_params=pltpu.CompilerParams(vmem_limit_bytes=LIMIT),
    )(slices)


def exchange(x, axes):
    return lax.all_to_all(x, axes, 0, 0)


def to_all(x, axes, n):
    return exchange(jnp.broadcast_to(x[None], (n,) + x.shape), axes)


def body(points, probes, near_list, near_count):
    leaf = ("y", "z", "c")
    size = lax.axis_size(leaf)
    rows = points.shape[0]
    packed = jnp.concatenate([probes, points], axis=1)
    up = [(i, i + 1) for i in range(size - 1)]
    below = lax.ppermute(packed, leaf, up).reshape(BLOCKS, BOX, 128)
    above = lax.ppermute(packed, leaf, [(b, a) for a, b in up]).reshape(BLOCKS, BOX, 128)
    own = packed.reshape(BLOCKS, BOX, 128)
    base = (lax.axis_index(leaf) * BLOCKS).astype(jnp.int32).reshape(1)
    partial = tiles(base, near_list, near_count, own, [own], [0])
    samples, send = tiles(
        base, near_list, near_count, own, [below, above], [-BLOCKS, BLOCKS], partial
    )
    columns = exchange(send, "x")
    pieces = gram(columns).reshape(8, 48, 128)
    level1 = jnp.sum(exchange(pieces, ("c", "x")), axis=0)
    along_z = to_all(level1, "z", 8)
    z = lax.axis_index("z")
    pair = lax.dynamic_slice_in_dim(along_z, z // 2 * 2, 2, 0)
    four = lax.dynamic_slice_in_dim(along_z, z // 4 * 4, 4, 0)
    level2 = jnp.sum(pair, axis=0)
    level3 = jnp.sum(four, axis=0)
    along_y = to_all(jnp.sum(along_z, axis=0), "y", 8)
    root = jnp.sum(along_y, axis=0)
    slices = to_all(jnp.stack([level1, level2, level3, root]), ("c", "x"), 8)
    scales = [1.0 / (rows * 2 ** (l + 1)) for l in range(LEVELS)] + [1.0 / (rows * size)]
    node_factors, root_factor = factors(slices, scales)
    return samples, node_factors, root_factor


def solution(mesh):
    fine = Mesh(mesh.devices.reshape(8, 8, 2, 4), ("y", "z", "c", "x"))
    leaf = ("y", "z", "c")
    return jax.shard_map(
        body,
        mesh=fine,
        in_specs=(P(leaf, None), P(leaf, "x"), P(leaf, None), P(leaf)),
        out_specs=(P(leaf, "x"), P(leaf, None, None, None), P()),
        check_vma=False,
    )
```

```python
import functools

import jax
import jax.numpy as jnp
from jax import lax
from jax.experimental import pallas as pl
from jax.experimental.pallas import tpu as pltpu
from jax.sharding import Mesh, PartitionSpec as P

LEVELS = 3
BLOCKS = 8
BOX = 256
SLOTS = 16
GROUP = 8
ENTRIES = BLOCKS * SLOTS + 3 * GROUP
BF = jnp.bfloat16
F = jnp.float32
NN = (((1,), (0,)), ((), ()))
NT = (((1,), (1,)), ((), ()))
TN = (((0,), (0,)), ((), ()))
LOG2E_OVER_32 = 1.4426950408889634 / 32.0
LIMIT = 20 << 20
VM = pl.BlockSpec(memory_space=pltpu.VMEM)
SM = pl.BlockSpec(memory_space=pltpu.SMEM)


def dot(a, b, dims):
    return lax.dot_general(a, b, dims, preferred_element_type=F)


def split3(x):
    h = x.astype(BF)
    r = x - h.astype(F)
    m = r.astype(BF)
    return h, m, (r - m.astype(F)).astype(BF)


def squared(box):
    wide = box[64:128].astype(F)
    sq = jnp.sum(wide * wide, axis=0, keepdims=True)
    h = sq.astype(BF).astype(F)
    m = (sq - h).astype(BF).astype(F)
    return h, m, sq - h - m, lax.broadcasted_iota(jnp.int32, (16, BOX), 0)


def extended(head, points):
    return jnp.concatenate([head.astype(BF), jnp.zeros((48, BOX), BF), points], axis=0)


def other_side(box):
    h, m, l, row = squared(box)
    head = jnp.where(row == 0, h, jnp.where(row == 1, m, jnp.where(row == 2, l, jnp.where(row < 6, 1.0, 0.0))))
    return extended(head, box[64:128]).T


def own_side(box):
    h, m, l, row = squared(box)
    head = jnp.where(row < 3, -1.0, jnp.where(row == 3, -h, jnp.where(row == 4, -m, jnp.where(row == 5, -l, 0.0))))
    return extended(head, (box[64:128].astype(F) * 2.0).astype(BF))


def build_lists(base, list_ref, count_ref, own, halo):
    def of_box(b, counts):
        def of_slot(s, counts):
            in_own, in_halo = counts
            j = list_ref[b, s] - base
            own[0, in_own] = b
            own[1, in_own] = j
            halo[0, in_halo] = b
            halo[1, in_halo] = jnp.where(j < 0, j + BLOCKS, j)
            inside = jnp.logical_and(j >= 0, j < BLOCKS).astype(jnp.int32)
            return in_own + inside, in_halo + 1 - inside

        return lax.fori_loop(0, count_ref[b], of_slot, counts)

    return lax.fori_loop(0, BLOCKS, of_box, (jnp.int32(GROUP), jnp.int32(GROUP)))


def run_list(end, ids, null, own, other, probes, cross, parts, total):
    for e in range(GROUP):
        ids[0, end + e] = 0
        ids[1, end + e] = null

    def step(t, _):
        at = [t * GROUP + k for k in range(GROUP)]
        for k in range(GROUP):
            cross[k] = dot(other[ids[1, at[k]]], own[ids[0, at[k]]], NN)
        for k in range(GROUP):
            tile = jnp.exp2(cross[k] * LOG2E_OVER_32)
            h = tile.astype(BF)
            parts[k, 0:BOX] = h
            parts[k, BOX:2 * BOX] = (tile - h.astype(F)).astype(BF)
        for k in range(GROUP):
            left = probes[ids[1, at[k]]]
            i = ids[0, at[k]]
            total[i] = total[i] + dot(jnp.concatenate([left, left], axis=1), parts[k], NN)
        return 0

    lax.fori_loop(1, (end + GROUP - 1) // GROUP, step, 0)


def own_kernel(base_ref, list_ref, count_ref, own_ref, total, sides, halo_ids, halo_end, other, probes, ids, cross, parts):
    end, halo_end[0] = build_lists(base_ref[0], list_ref, count_ref, ids, halo_ids)
    for b in range(BLOCKS):
        box = own_ref[:, BOX * b:BOX * b + BOX]
        other[b] = other_side(box)
        sides[b] = own_side(box)
        probes[b] = box[0:64]
    other[BLOCKS] = jnp.zeros((BOX, 128), BF)
    probes[BLOCKS] = jnp.zeros((64, BOX), BF)
    total[...] = jnp.zeros_like(total)
    run_list(end, ids, BLOCKS, sides, other, probes, cross, parts, total)


def halo_kernel(ids_ref, end_ref, below_ref, above_ref, sides, part, turned, send, other, probes, ids, cross, parts, total):
    end = end_ref[0]

    def keep(e, _):
        ids[0, e] = ids_ref[0, e]
        ids[1, e] = ids_ref[1, e]
        return 0

    lax.fori_loop(GROUP, end, keep, 0)
    for q, ref in enumerate((below_ref, above_ref)):
        for b in range(BLOCKS):
            box = ref[:, BOX * b:BOX * b + BOX]
            other[BLOCKS * q + b] = other_side(box)
            probes[BLOCKS * q + b] = box[0:64]
    other[2 * BLOCKS] = jnp.zeros((BOX, 128), BF)
    probes[2 * BLOCKS] = jnp.zeros((64, BOX), BF)
    total[...] = part[...]
    run_list(end, ids, 2 * BLOCKS, sides, other, probes, cross, parts, total)
    for b in range(BLOCKS):
        turned[:, BOX * b:BOX * b + BOX] = total[b]
        send[b // 2, b % 2] = total[b]


def list_scratch(boxes):
    return [
        pltpu.VMEM((boxes + 1, BOX, 128), BF),
        pltpu.VMEM((boxes + 1, 64, BOX), BF),
        pltpu.SMEM((2, ENTRIES), jnp.int32),
        pltpu.VMEM((GROUP, BOX, BOX), F),
        pltpu.VMEM((GROUP, 2 * BOX, BOX), BF),
    ]


def tiles_cost():
    return pl.CostEstimate(
        flops=64 * 3 * BOX * BOX * 128 * 2, bytes_accessed=4 << 20, transcendentals=64 * BOX * BOX
    )


def own_tiles(base, near_list, near_count, own):
    return pl.pallas_call(
        own_kernel,
        out_shape=(
            jax.ShapeDtypeStruct((BLOCKS, 64, BOX), F),
            jax.ShapeDtypeStruct((BLOCKS, 128, BOX), BF),
            jax.ShapeDtypeStruct((2, ENTRIES), jnp.int32),
            jax.ShapeDtypeStruct((1,), jnp.int32),
        ),
        in_specs=[SM, SM, SM, VM],
        out_specs=(VM, VM, SM, SM),
        scratch_shapes=list_scratch(BLOCKS),
        compiler_params=pltpu.CompilerParams(vmem_limit_bytes=LIMIT),
        cost_estimate=tiles_cost(),
    )(base, near_list, near_count, own)


def halo_tiles(ids, end, below, above, sides, part):
    return pl.pallas_call(
        halo_kernel,
        out_shape=(
            jax.ShapeDtypeStruct((64, BLOCKS * BOX), F),
            jax.ShapeDtypeStruct((BLOCKS // 2, 2, 64, BOX), F),
        ),
        in_specs=[SM, SM] + [VM] * 4,
        out_specs=(VM, VM),
        scratch_shapes=list_scratch(2 * BLOCKS) + [pltpu.VMEM((BLOCKS, 64, BOX), F)],
        compiler_params=pltpu.CompilerParams(vmem_limit_bytes=LIMIT),
        cost_estimate=tiles_cost(),
    )(ids, end, below, above, sides, part)


def gram_kernel(columns_ref, out_ref):
    g = None
    for b in range(2):
        h, m, l = split3(jnp.concatenate([columns_ref[q, b] for q in range(4)], axis=0))
        left = jnp.concatenate([h, h, m, h, m, l], axis=1)
        right = jnp.concatenate([h, m, h, l, m, h], axis=1)
        term = dot(left, right, NT)
        g = term if g is None else g + term
    out_ref[0:128, :] = g[0:128, 0:128]
    out_ref[128:256, :] = g[0:128, 128:256]
    out_ref[256:384, :] = g[128:256, 128:256]


def gram(columns):
    return pl.pallas_call(
        gram_kernel,
        out_shape=jax.ShapeDtypeStruct((384, 128), F),
        in_specs=[VM],
        out_specs=VM,
        compiler_params=pltpu.CompilerParams(vmem_limit_bytes=LIMIT),
    )(columns)


def panel_step(rows, off, width):
    n = len(rows)
    lanes = range(width // 128)
    sub = lax.broadcasted_iota(jnp.int32, (8, 128), 0)
    part = [[[r[8 * g:8 * g + 8, 128 * q:128 * q + 128] for q in lanes] for g in range(4)] for r in rows]
    for s in range(4):
        at = off + 8 * s
        cols = [
            [
                None if g < s else [
                    jnp.broadcast_to(part[b][g][0][:, at + j:at + j + 1], (8, 128)) for j in range(8)
                ]
                for g in range(4)
            ]
            for b in range(n)
        ]
        scale = [None] * n
        for j in range(8):
            for b in range(n):
                here = cols[b][s]
                pivot = jnp.broadcast_to(here[j][j:j + 1, :], (8, 128))
                inverse = 1.0 / pivot
                root = lax.rsqrt(pivot)
                scale[b] = root if j == 0 else jnp.where(sub == j, root, scale[b])
                ratio = [
                    None if l <= j else jnp.broadcast_to(here[l][j:j + 1, :], (8, 128)) * inverse
                    for l in range(8)
                ]
                row = [jnp.broadcast_to(part[b][s][q][j:j + 1, :], (8, 128)) * inverse for q in lanes]
                for g in range(s, 4):
                    c = cols[b][g][j]
                    for l in range(j + 1, 8):
                        cols[b][g][l] = cols[b][g][l] - c * ratio[l]
                    if g == s:
                        c = jnp.where(sub > j, c, 0.0)
                    part[b][g] = [part[b][g][q] - c * row[q] for q in lanes]
        for b in range(n):
            part[b][s] = [v * scale[b] for v in part[b][s]]
    return [jnp.concatenate([jnp.concatenate(v, axis=1) for v in p], axis=0) for p in part]


def factor(n, work, upper):
    for half in range(2):
        c0 = 128 * half
        for k in range(4):
            r0 = c0 + 32 * k
            rows = panel_step([work[b, r0:r0 + 32, c0:256] for b in range(n)], 32 * k, 256 - c0)
            for b in range(n):
                upper[b, r0:r0 + 32, c0:256] = rows[b]
            lo = r0 + 32
            if lo == 256:
                break
            for b in range(n):
                h, m, l = split3(rows[b])
                left = jnp.concatenate([h, h, m, h, m, l], axis=0)
                right = jnp.concatenate([h, m, h, l, m, h], axis=0)
                work[b, lo:256, c0:256] = work[b, lo:256, c0:256] - dot(left, right, TN)[lo - c0:, :]


def factor_kernel(scales, slices_ref, nodes_ref, root_ref, work, upper):
    n = len(scales)
    ri = lax.broadcasted_iota(jnp.int32, (128, 128), 0)
    ci = lax.broadcasted_iota(jnp.int32, (128, 128), 1)
    eye = jnp.where(ri == ci, 1.0, 0.0)
    for b in range(n):
        tri = jnp.concatenate([slices_ref[r, b] for r in range(8)], axis=0) * scales[b]
        work[b, 0:128, 0:128] = tri[0:128] + eye
        work[b, 0:128, 128:256] = tri[128:256]
        work[b, 128:256, 0:128] = jnp.zeros((128, 128), F)
        work[b, 128:256, 128:256] = tri[256:384] + eye
        upper[b, 128:256, 0:128] = jnp.zeros((128, 128), F)
    factor(n, work, upper)
    rows = lax.broadcasted_iota(jnp.int32, (256, 256), 0)
    cols = lax.broadcasted_iota(jnp.int32, (256, 256), 1)
    for b in range(n):
        low = jnp.where(rows >= cols, upper[b].T, 0.0)
        if b < LEVELS:
            nodes_ref[0, b] = low
        else:
            root_ref[...] = low


def factors(slices, scales):
    n = len(scales)
    return pl.pallas_call(
        functools.partial(factor_kernel, scales),
        out_shape=(
            jax.ShapeDtypeStruct((1, LEVELS, 256, 256), F),
            jax.ShapeDtypeStruct((256, 256), F),
        ),
        in_specs=[VM],
        out_specs=(VM, VM),
        scratch_shapes=[pltpu.VMEM((n, 256, 256), F)] * 2,
        compiler_params=pltpu.CompilerParams(vmem_limit_bytes=LIMIT),
    )(slices)


def exchange(x, axes):
    return lax.all_to_all(x, axes, 0, 0)


def to_all(x, axes, n):
    return exchange(jnp.broadcast_to(x[None], (n,) + x.shape), axes)


def body(points, probes, near_list, near_count):
    leaf = ("y", "z", "c")
    size = lax.axis_size(leaf)
    rows = points.shape[0]
    packed = jnp.concatenate([probes.T, points.T], axis=0)
    up = [(i, i + 1) for i in range(size - 1)]
    below = lax.ppermute(packed, leaf, up)
    above = lax.ppermute(packed, leaf, [(b, a) for a, b in up])
    base = (lax.axis_index(leaf) * BLOCKS).astype(jnp.int32).reshape(1)
    part, sides, ids, end = own_tiles(base, near_list, near_count, packed)
    turned, send = halo_tiles(ids, end, below, above, sides, part)
    samples = turned.T
    columns = exchange(send, "x")
    pieces = gram(columns).reshape(8, 48, 128)
    level1 = jnp.sum(exchange(pieces, ("c", "x")), axis=0)
    along_z = to_all(level1, "z", 8)
    z = lax.axis_index("z")
    pair = lax.dynamic_slice_in_dim(along_z, z // 2 * 2, 2, 0)
    four = lax.dynamic_slice_in_dim(along_z, z // 4 * 4, 4, 0)
    level2 = jnp.sum(pair, axis=0)
    level3 = jnp.sum(four, axis=0)
    along_y = to_all(jnp.sum(along_z, axis=0), "y", 8)
    root = jnp.sum(along_y, axis=0)
    slices = to_all(jnp.stack([level1, level2, level3, root]), ("c", "x"), 8)
    scales = [1.0 / (rows * 2 ** (l + 1)) for l in range(LEVELS)] + [1.0 / (rows * size)]
    node_factors, root_factor = factors(slices, scales)
    return samples, node_factors, root_factor


def solution(mesh):
    fine = Mesh(mesh.devices.reshape(8, 8, 2, 4), ("y", "z", "c", "x"))
    leaf = ("y", "z", "c")
    return jax.shard_map(
        body,
        mesh=fine,
        in_specs=(P(leaf, None), P(leaf, "x"), P(leaf, None), P(leaf)),
        out_specs=(P(leaf, "x"), P(leaf, None, None, None), P()),
        check_vma=False,
    )
```

```python
import functools

import jax
import jax.numpy as jnp
from jax import lax
from jax.experimental import pallas as pl
from jax.experimental.pallas import tpu as pltpu
from jax.sharding import Mesh, PartitionSpec as P

LEVELS = 3
BLOCKS = 8
BOX = 256
SLOTS = 16
GROUP = 8
ENTRIES = BLOCKS * SLOTS + 3 * GROUP
BF = jnp.bfloat16
F = jnp.float32
NN = (((1,), (0,)), ((), ()))
NT = (((1,), (1,)), ((), ()))
TN = (((0,), (0,)), ((), ()))
LOG2E_OVER_32 = 1.4426950408889634 / 32.0
LIMIT = 20 << 20
VM = pl.BlockSpec(memory_space=pltpu.VMEM)
SM = pl.BlockSpec(memory_space=pltpu.SMEM)


def dot(a, b, dims):
    return lax.dot_general(a, b, dims, preferred_element_type=F)


def split3(x):
    h = x.astype(BF)
    r = x - h.astype(F)
    m = r.astype(BF)
    return h, m, (r - m.astype(F)).astype(BF)


def squared(box):
    wide = box[64:128].astype(F)
    sq = jnp.sum(wide * wide, axis=0, keepdims=True)
    h = sq.astype(BF).astype(F)
    m = (sq - h).astype(BF).astype(F)
    return h, m, sq - h - m, lax.broadcasted_iota(jnp.int32, (16, BOX), 0)


def extended(head, points):
    return jnp.concatenate([head.astype(BF), jnp.zeros((48, BOX), BF), points], axis=0)


def other_side(box):
    h, m, l, row = squared(box)
    head = jnp.where(row == 0, h, jnp.where(row == 1, m, jnp.where(row == 2, l, jnp.where(row < 6, 1.0, 0.0))))
    return extended(head, box[64:128]).T


def own_side(box):
    h, m, l, row = squared(box)
    head = jnp.where(row < 3, -1.0, jnp.where(row == 3, -h, jnp.where(row == 4, -m, jnp.where(row == 5, -l, 0.0))))
    return extended(head, (box[64:128].astype(F) * 2.0).astype(BF))


def build_lists(base, list_ref, count_ref, own, halo):
    def of_box(b, counts):
        def of_slot(s, counts):
            in_own, in_halo = counts
            j = list_ref[b, s] - base
            own[0, in_own] = b
            own[1, in_own] = j
            halo[0, in_halo] = b
            halo[1, in_halo] = jnp.where(j < 0, j + BLOCKS, j)
            inside = jnp.logical_and(j >= 0, j < BLOCKS).astype(jnp.int32)
            return in_own + inside, in_halo + 1 - inside

        return lax.fori_loop(0, count_ref[b], of_slot, counts)

    return lax.fori_loop(0, BLOCKS, of_box, (jnp.int32(GROUP), jnp.int32(GROUP)))


def run_list(end, ids, own, other, probes, cross, parts, total):
    def step(t, _):
        at = [t * GROUP + k for k in range(GROUP)]
        for k in range(GROUP):
            cross[k] = dot(other[ids[1, at[k]]], own[ids[0, at[k]]], NN)
        for k in range(GROUP):
            tile = jnp.exp2(cross[k] * LOG2E_OVER_32)
            h = tile.astype(BF)
            parts[k, 0:BOX] = h
            parts[k, BOX:2 * BOX] = (tile - h.astype(F)).astype(BF)
        for k in range(GROUP):
            left = probes[ids[1, at[k]]]
            i = ids[0, at[k]]
            total[i] = total[i] + dot(jnp.concatenate([left, left], axis=1), parts[k], NN)
        return 0

    lax.fori_loop(1, (end + GROUP - 1) // GROUP, step, 0)


def own_kernel(
    base_ref, list_hbm, count_hbm, own_ref, total, sides, halo_ids, halo_end,
    other, probes, cross, parts, ids, list_ref, count_ref, sems,
):
    copies = [
        pltpu.make_async_copy(list_hbm, list_ref, sems.at[0]),
        pltpu.make_async_copy(count_hbm, count_ref, sems.at[1]),
    ]
    for copy in copies:
        copy.start()
    for b in range(BLOCKS):
        box = own_ref[:, BOX * b:BOX * b + BOX]
        other[b] = other_side(box)
        sides[b] = own_side(box)
        probes[b] = box[0:64]
    other[BLOCKS] = jnp.zeros((BOX, 128), BF)
    probes[BLOCKS] = jnp.zeros((64, BOX), BF)
    total[...] = jnp.zeros_like(total)
    for copy in copies:
        copy.wait()
    end, end_halo = build_lists(base_ref[0], list_ref, count_ref, ids, halo_ids)
    halo_end[0] = end_halo
    for k in range(GROUP):
        ids[0, end + k] = 0
        ids[1, end + k] = BLOCKS
        halo_ids[0, end_halo + k] = 0
        halo_ids[1, end_halo + k] = 2 * BLOCKS
    run_list(end, ids, sides, other, probes, cross, parts, total)


def halo_kernel(ids, end_ref, below_ref, above_ref, sides, part, turned, send, other, probes, cross, parts, total):
    for q, ref in enumerate((below_ref, above_ref)):
        for b in range(BLOCKS):
            box = ref[:, BOX * b:BOX * b + BOX]
            other[BLOCKS * q + b] = other_side(box)
            probes[BLOCKS * q + b] = box[0:64]
    other[2 * BLOCKS] = jnp.zeros((BOX, 128), BF)
    probes[2 * BLOCKS] = jnp.zeros((64, BOX), BF)
    total[...] = part[...]
    run_list(end_ref[0], ids, sides, other, probes, cross, parts, total)
    for b in range(BLOCKS):
        turned[:, BOX * b:BOX * b + BOX] = total[b]
        send[b // 2, b % 2] = total[b]


def list_scratch(boxes):
    return [
        pltpu.VMEM((boxes + 1, BOX, 128), BF),
        pltpu.VMEM((boxes + 1, 64, BOX), BF),
        pltpu.VMEM((GROUP, BOX, BOX), F),
        pltpu.VMEM((GROUP, 2 * BOX, BOX), BF),
    ]


def tiles_cost():
    return pl.CostEstimate(
        flops=64 * 3 * BOX * BOX * 128 * 2, bytes_accessed=4 << 20, transcendentals=64 * BOX * BOX
    )


def own_tiles(base, near_list, near_count, own):
    return pl.pallas_call(
        own_kernel,
        out_shape=(
            jax.ShapeDtypeStruct((BLOCKS, 64, BOX), F),
            jax.ShapeDtypeStruct((BLOCKS, 128, BOX), BF),
            jax.ShapeDtypeStruct((2, ENTRIES), jnp.int32),
            jax.ShapeDtypeStruct((1,), jnp.int32),
        ),
        in_specs=[SM, pl.BlockSpec(memory_space=pltpu.HBM), pl.BlockSpec(memory_space=pltpu.HBM), VM],
        out_specs=(VM, VM, SM, SM),
        scratch_shapes=list_scratch(BLOCKS)
        + [
            pltpu.SMEM((2, ENTRIES), jnp.int32),
            pltpu.SMEM((BLOCKS, SLOTS), jnp.int32),
            pltpu.SMEM((BLOCKS,), jnp.int32),
            pltpu.SemaphoreType.DMA((2,)),
        ],
        compiler_params=pltpu.CompilerParams(vmem_limit_bytes=LIMIT),
        cost_estimate=tiles_cost(),
    )(base, near_list, near_count, own)


def halo_tiles(ids, end, below, above, sides, part):
    return pl.pallas_call(
        halo_kernel,
        out_shape=(
            jax.ShapeDtypeStruct((64, BLOCKS * BOX), F),
            jax.ShapeDtypeStruct((BLOCKS // 2, 2, 64, BOX), F),
        ),
        in_specs=[SM, SM] + [VM] * 4,
        out_specs=(VM, VM),
        scratch_shapes=list_scratch(2 * BLOCKS) + [pltpu.VMEM((BLOCKS, 64, BOX), F)],
        compiler_params=pltpu.CompilerParams(vmem_limit_bytes=LIMIT),
        cost_estimate=tiles_cost(),
    )(ids, end, below, above, sides, part)


def gram_kernel(columns_ref, out_ref):
    g = None
    for b in range(2):
        h, m, l = split3(jnp.concatenate([columns_ref[q, b] for q in range(4)], axis=0))
        left = jnp.concatenate([h, h, m, h, m, l], axis=1)
        right = jnp.concatenate([h, m, h, l, m, h], axis=1)
        term = dot(left, right, NT)
        g = term if g is None else g + term
    out_ref[0:64, :] = g[0:64, 0:128]
    out_ref[64:128, :] = g[0:64, 128:256]
    out_ref[128:192, :] = g[64:128, 128:256]
    out_ref[192:256, :] = g[128:192, 128:256]
    low_lanes = lax.broadcasted_iota(jnp.int32, (64, 128), 1) < 64
    out_ref[256:320, :] = jnp.where(low_lanes, pltpu.roll(g[192:256, 128:256], 64, 1), g[64:128, 0:128])


def gram(columns):
    return pl.pallas_call(
        gram_kernel,
        out_shape=jax.ShapeDtypeStruct((320, 128), F),
        in_specs=[VM],
        out_specs=VM,
        compiler_params=pltpu.CompilerParams(vmem_limit_bytes=LIMIT),
    )(columns)


def lane_of(x, lane):
    index = jnp.full((8, 128, 1), lane, jnp.int32)
    dims = lax.GatherDimensionNumbers(
        offset_dims=(),
        collapsed_slice_dims=(1,),
        start_index_map=(1,),
        operand_batching_dims=(0,),
        start_indices_batching_dims=(0,),
    )
    return lax.gather(x, index, dims, (1, 1), mode=lax.GatherScatterMode.PROMISE_IN_BOUNDS)


def panel_step(rows, off, width):
    n = len(rows)
    lanes = range(width // 128)
    sub = lax.broadcasted_iota(jnp.int32, (8, 128), 0)
    part = [[[r[8 * g:8 * g + 8, 128 * q:128 * q + 128] for q in lanes] for g in range(4)] for r in rows]
    for s in range(4):
        at = off + 8 * s
        cols = [
            [None if g < s else [lane_of(part[b][g][0], at + j) for j in range(8)] for g in range(4)]
            for b in range(n)
        ]
        pivots = [None] * n
        for j in range(8):
            for b in range(n):
                here = cols[b][s]
                pivot = jnp.broadcast_to(here[j][j:j + 1, :], (8, 128))
                inverse = 1.0 / pivot
                pivots[b] = pivot if j == 0 else jnp.where(sub == j, pivot, pivots[b])
                if j == 7 and s == 3:
                    continue
                ratio = [
                    None if l <= j else jnp.broadcast_to(here[l][j:j + 1, :], (8, 128)) * inverse
                    for l in range(8)
                ]
                row = [jnp.broadcast_to(part[b][s][q][j:j + 1, :], (8, 128)) * inverse for q in lanes]
                for g in range(s, 4):
                    if g == s and j == 7:
                        continue
                    c = cols[b][g][j]
                    for l in range(j + 1, 8):
                        cols[b][g][l] = cols[b][g][l] - c * ratio[l]
                    if g == s:
                        c = jnp.where(sub > j, c, 0.0)
                    part[b][g] = [part[b][g][q] - c * row[q] for q in lanes]
        for b in range(n):
            scale = lax.rsqrt(pivots[b])
            part[b][s] = [v * scale for v in part[b][s]]
    return [jnp.concatenate([jnp.concatenate(v, axis=1) for v in p], axis=0) for p in part]


def factor(n, work, upper):
    for half in range(2):
        c0 = 128 * half
        for k in range(4):
            r0 = c0 + 32 * k
            rows = panel_step([work[b, r0:r0 + 32, c0:256] for b in range(n)], 32 * k, 256 - c0)
            for b in range(n):
                upper[b, r0:r0 + 32, c0:256] = rows[b]
            lo = r0 + 32
            if lo == 256:
                break
            for b in range(n):
                h, m, l = split3(rows[b])
                left = jnp.concatenate([h, h, m, h, m, l], axis=0)
                right = jnp.concatenate([h, m, h, l, m, h], axis=0)
                update = dot(left, right, TN)
                if half == 0:
                    if lo < 128:
                        work[b, lo:128, :] = work[b, lo:128, :] - update[lo:128, :]
                    work[b, 128:256, 128:256] = work[b, 128:256, 128:256] - update[128:256, 128:256]
                else:
                    work[b, lo:256, 128:256] = work[b, lo:256, 128:256] - update[lo - 128:128, :]


def factor_kernel(scales, slices_ref, nodes_ref, root_ref, work, upper):
    n = len(scales)
    ri = lax.broadcasted_iota(jnp.int32, (128, 128), 0)
    ci = lax.broadcasted_iota(jnp.int32, (128, 128), 1)
    eye = jnp.where(ri == ci, 1.0, 0.0)
    for b in range(n):
        t = jnp.concatenate([slices_ref[r, b] for r in range(8)], axis=0) * scales[b]
        work[b, 0:64, 0:128] = t[0:64] + eye[0:64]
        work[b, 0:64, 128:256] = t[64:128]
        work[b, 64:128, 0:128] = t[256:320] + eye[64:128]
        work[b, 64:128, 128:256] = t[128:192]
        work[b, 128:192, 128:256] = t[192:256] + eye[0:64]
        work[b, 192:256, 128:256] = pltpu.roll(t[256:320], 64, 1) + eye[64:128]
    factor(n, work, upper)
    below = ri >= ci
    for b in range(n):
        first = jnp.where(below, upper[b, 0:128, 0:128].T, 0.0)
        cross = upper[b, 0:128, 128:256].T
        second = jnp.where(below, upper[b, 128:256, 128:256].T, 0.0)
        low = jnp.concatenate(
            [
                jnp.concatenate([first, jnp.zeros((128, 128), F)], axis=1),
                jnp.concatenate([cross, second], axis=1),
            ],
            axis=0,
        )
        if b < LEVELS:
            nodes_ref[0, b] = low
        else:
            root_ref[...] = low


def factors(slices, scales):
    n = len(scales)
    return pl.pallas_call(
        functools.partial(factor_kernel, scales),
        out_shape=(
            jax.ShapeDtypeStruct((1, LEVELS, 256, 256), F),
            jax.ShapeDtypeStruct((256, 256), F),
        ),
        in_specs=[VM],
        out_specs=(VM, VM),
        scratch_shapes=[pltpu.VMEM((n, 256, 256), F)] * 2,
        compiler_params=pltpu.CompilerParams(vmem_limit_bytes=LIMIT),
    )(slices)


def exchange(x, axes):
    return lax.all_to_all(x, axes, 0, 0)


def to_all(x, axes, n):
    return exchange(jnp.broadcast_to(x[None], (n,) + x.shape), axes)


def body(points, probes, near_list, near_count):
    leaf = ("y", "z", "c")
    size = lax.axis_size(leaf)
    rows = points.shape[0]
    packed = jnp.concatenate([probes.T, points.T], axis=0)
    up = [(i, i + 1) for i in range(size - 1)]
    below = lax.ppermute(packed, leaf, up)
    above = lax.ppermute(packed, leaf, [(b, a) for a, b in up])
    base = (lax.axis_index(leaf) * BLOCKS).astype(jnp.int32).reshape(1)
    part, sides, ids, end = own_tiles(base, near_list, near_count, packed)
    turned, send = halo_tiles(ids, end, below, above, sides, part)
    samples = turned.T
    columns = exchange(send, "x")
    pieces = gram(columns).reshape(8, 40, 128)
    level1 = jnp.sum(exchange(pieces, ("c", "x")), axis=0)
    along_z = to_all(level1, "z", 8)
    z = lax.axis_index("z")
    pair = lax.dynamic_slice_in_dim(along_z, z // 2 * 2, 2, 0)
    four = lax.dynamic_slice_in_dim(along_z, z // 4 * 4, 4, 0)
    level2 = jnp.sum(pair, axis=0)
    level3 = jnp.sum(four, axis=0)
    line = jnp.sum(along_z, axis=0)
    level2, level3, line = lax.optimization_barrier((level2, level3, line))
    along_y = to_all(line, "y", 8)
    root = jnp.sum(along_y, axis=0)
    slices = to_all(jnp.stack([level1, level2, level3, root]), ("c", "x"), 8)
    scales = [1.0 / (rows * 2 ** (l + 1)) for l in range(LEVELS)] + [1.0 / (rows * size)]
    node_factors, root_factor = factors(slices, scales)
    return samples, node_factors, root_factor


def solution(mesh):
    fine = Mesh(mesh.devices.reshape(8, 8, 2, 4), ("y", "z", "c", "x"))
    leaf = ("y", "z", "c")
    return jax.shard_map(
        body,
        mesh=fine,
        in_specs=(P(leaf, None), P(leaf, "x"), P(leaf, None), P(leaf)),
        out_specs=(P(leaf, "x"), P(leaf, None, None, None), P()),
        check_vma=False,
    )
```

```python
import functools

import jax
import jax.numpy as jnp
from jax import lax
from jax.experimental import pallas as pl
from jax.experimental.pallas import tpu as pltpu
from jax.sharding import Mesh, PartitionSpec as P

LEVELS = 3
BLOCKS = 8
BOX = 256
SLOTS = 16
GROUP = 8
ENTRIES = BLOCKS * SLOTS + 3 * GROUP
BF = jnp.bfloat16
F = jnp.float32
NN = (((1,), (0,)), ((), ()))
NT = (((1,), (1,)), ((), ()))
TN = (((0,), (0,)), ((), ()))
LOG2E_OVER_32 = 1.4426950408889634 / 32.0
LIMIT = 20 << 20
VM = pl.BlockSpec(memory_space=pltpu.VMEM)
SM = pl.BlockSpec(memory_space=pltpu.SMEM)


def dot(a, b, dims):
    return lax.dot_general(a, b, dims, preferred_element_type=F)


def split3(x):
    h = x.astype(BF)
    r = x - h.astype(F)
    m = r.astype(BF)
    return h, m, (r - m.astype(F)).astype(BF)


def squared(box):
    wide = box[64:128].astype(F)
    sq = jnp.sum(wide * wide, axis=0, keepdims=True)
    h = sq.astype(BF).astype(F)
    m = (sq - h).astype(BF).astype(F)
    return h, m, sq - h - m, lax.broadcasted_iota(jnp.int32, (16, BOX), 0)


def extended(head, points):
    return jnp.concatenate([head.astype(BF), jnp.zeros((48, BOX), BF), points], axis=0)


def other_side(box):
    h, m, l, row = squared(box)
    head = jnp.where(row == 0, h, jnp.where(row == 1, m, jnp.where(row == 2, l, jnp.where(row < 6, 1.0, 0.0))))
    return extended(head, box[64:128]).T


def own_side(box):
    h, m, l, row = squared(box)
    head = jnp.where(row < 3, -1.0, jnp.where(row == 3, -h, jnp.where(row == 4, -m, jnp.where(row == 5, -l, 0.0))))
    return extended(head, (box[64:128].astype(F) * 2.0).astype(BF))


def build_lists(base, list_ref, count_ref, own, halo):
    core = (base // BLOCKS) % 2

    def of_box(b, counts):
        def of_slot(s, counts):
            in_own, in_halo = counts
            j = list_ref[b, s] - base
            own[0, in_own] = b
            own[1, in_own] = j
            halo[0, in_halo] = b
            before = (j < 0).astype(jnp.int32)
            halo[1, in_halo] = jnp.where(j < 0, j + BLOCKS, j - BLOCKS) + BLOCKS * (before ^ core)
            inside = jnp.logical_and(j >= 0, j < BLOCKS).astype(jnp.int32)
            return in_own + inside, in_halo + 1 - inside

        return lax.fori_loop(0, count_ref[b], of_slot, counts)

    return lax.fori_loop(0, BLOCKS, of_box, (jnp.int32(GROUP), jnp.int32(GROUP)))


def run_list(end, ids, own, other, probes, cross, parts, total):
    def step(t, _):
        at = [t * GROUP + k for k in range(GROUP)]
        for k in range(GROUP):
            cross[k] = dot(other[ids[1, at[k]]], own[ids[0, at[k]]], NN)
        for k in range(GROUP):
            tile = jnp.exp2(cross[k] * LOG2E_OVER_32)
            h = tile.astype(BF)
            parts[k, 0:BOX] = h
            parts[k, BOX:2 * BOX] = (tile - h.astype(F)).astype(BF)
        for k in range(GROUP):
            left = probes[ids[1, at[k]]]
            i = ids[0, at[k]]
            total[i] = total[i] + dot(jnp.concatenate([left, left], axis=1), parts[k], NN)
        return 0

    lax.fori_loop(1, (end + GROUP - 1) // GROUP, step, 0)


def own_kernel(
    base_ref, list_hbm, count_hbm, own_ref, total, sides, halo_ids, halo_end,
    other, probes, cross, parts, ids, list_ref, count_ref, sems,
):
    copies = [
        pltpu.make_async_copy(list_hbm, list_ref, sems.at[0]),
        pltpu.make_async_copy(count_hbm, count_ref, sems.at[1]),
    ]
    for copy in copies:
        copy.start()
    for b in range(BLOCKS):
        box = own_ref[:, BOX * b:BOX * b + BOX]
        other[b] = other_side(box)
        sides[b] = own_side(box)
        probes[b] = box[0:64]
    other[BLOCKS] = jnp.zeros((BOX, 128), BF)
    probes[BLOCKS] = jnp.zeros((64, BOX), BF)
    total[...] = jnp.zeros_like(total)
    for copy in copies:
        copy.wait()
    end, end_halo = build_lists(base_ref[0], list_ref, count_ref, ids, halo_ids)
    halo_end[0] = end_halo
    for k in range(GROUP):
        ids[0, end + k] = 0
        ids[1, end + k] = BLOCKS
        halo_ids[0, end_halo + k] = 0
        halo_ids[1, end_halo + k] = 2 * BLOCKS
    run_list(end, ids, sides, other, probes, cross, parts, total)


def halo_kernel(ids, end_ref, near_ref, far_ref, sides, part, turned, send, other, probes, cross, parts, total):
    for q, ref in enumerate((near_ref, far_ref)):
        for b in range(BLOCKS):
            box = ref[:, BOX * b:BOX * b + BOX]
            other[BLOCKS * q + b] = other_side(box)
            probes[BLOCKS * q + b] = box[0:64]
    other[2 * BLOCKS] = jnp.zeros((BOX, 128), BF)
    probes[2 * BLOCKS] = jnp.zeros((64, BOX), BF)
    total[...] = part[...]
    run_list(end_ref[0], ids, sides, other, probes, cross, parts, total)
    for b in range(BLOCKS):
        turned[:, BOX * b:BOX * b + BOX] = total[b]
        send[b // 2, b % 2] = total[b]


def list_scratch(boxes):
    return [
        pltpu.VMEM((boxes + 1, BOX, 128), BF),
        pltpu.VMEM((boxes + 1, 64, BOX), BF),
        pltpu.VMEM((GROUP, BOX, BOX), F),
        pltpu.VMEM((GROUP, 2 * BOX, BOX), BF),
    ]


def tiles_cost():
    return pl.CostEstimate(
        flops=64 * 3 * BOX * BOX * 128 * 2, bytes_accessed=4 << 20, transcendentals=64 * BOX * BOX
    )


def own_tiles(base, near_list, near_count, own):
    return pl.pallas_call(
        own_kernel,
        out_shape=(
            jax.ShapeDtypeStruct((BLOCKS, 64, BOX), F),
            jax.ShapeDtypeStruct((BLOCKS, 128, BOX), BF),
            jax.ShapeDtypeStruct((2, ENTRIES), jnp.int32),
            jax.ShapeDtypeStruct((1,), jnp.int32),
        ),
        in_specs=[SM, pl.BlockSpec(memory_space=pltpu.HBM), pl.BlockSpec(memory_space=pltpu.HBM), VM],
        out_specs=(VM, VM, SM, SM),
        scratch_shapes=list_scratch(BLOCKS)
        + [
            pltpu.SMEM((2, ENTRIES), jnp.int32),
            pltpu.SMEM((BLOCKS, SLOTS), jnp.int32),
            pltpu.SMEM((BLOCKS,), jnp.int32),
            pltpu.SemaphoreType.DMA((2,)),
        ],
        compiler_params=pltpu.CompilerParams(vmem_limit_bytes=LIMIT),
        cost_estimate=tiles_cost(),
    )(base, near_list, near_count, own)


def halo_tiles(ids, end, near, far, sides, part):
    return pl.pallas_call(
        halo_kernel,
        out_shape=(
            jax.ShapeDtypeStruct((64, BLOCKS * BOX), F),
            jax.ShapeDtypeStruct((BLOCKS // 2, 2, 64, BOX), F),
        ),
        in_specs=[SM, SM] + [VM] * 4,
        out_specs=(VM, VM),
        scratch_shapes=list_scratch(2 * BLOCKS) + [pltpu.VMEM((BLOCKS, 64, BOX), F)],
        compiler_params=pltpu.CompilerParams(vmem_limit_bytes=LIMIT),
        cost_estimate=tiles_cost(),
    )(ids, end, near, far, sides, part)


def gram_kernel(columns_ref, out_ref):
    g = None
    for b in range(2):
        h, m, l = split3(jnp.concatenate([columns_ref[q, b] for q in range(4)], axis=0))
        left = jnp.concatenate([h, h, m, h, m, l], axis=1)
        right = jnp.concatenate([h, m, h, l, m, h], axis=1)
        term = dot(left, right, NT)
        g = term if g is None else g + term
    out_ref[0:64, :] = g[0:64, 0:128]
    out_ref[64:128, :] = g[0:64, 128:256]
    out_ref[128:192, :] = g[64:128, 128:256]
    out_ref[192:256, :] = g[128:192, 128:256]
    low_lanes = lax.broadcasted_iota(jnp.int32, (64, 128), 1) < 64
    out_ref[256:320, :] = jnp.where(low_lanes, pltpu.roll(g[192:256, 128:256], 64, 1), g[64:128, 0:128])


def gram(columns):
    return pl.pallas_call(
        gram_kernel,
        out_shape=jax.ShapeDtypeStruct((320, 128), F),
        in_specs=[VM],
        out_specs=VM,
        compiler_params=pltpu.CompilerParams(vmem_limit_bytes=LIMIT),
    )(columns)


def lane_of(x, lane):
    index = jnp.full((8, 128, 1), lane, jnp.int32)
    dims = lax.GatherDimensionNumbers(
        offset_dims=(),
        collapsed_slice_dims=(1,),
        start_index_map=(1,),
        operand_batching_dims=(0,),
        start_indices_batching_dims=(0,),
    )
    return lax.gather(x, index, dims, (1, 1), mode=lax.GatherScatterMode.PROMISE_IN_BOUNDS)


def panel_step(rows, off, width):
    n = len(rows)
    lanes = range(width // 128)
    sub = lax.broadcasted_iota(jnp.int32, (8, 128), 0)
    part = [[[r[8 * g:8 * g + 8, 128 * q:128 * q + 128] for q in lanes] for g in range(4)] for r in rows]
    for s in range(4):
        at = off + 8 * s
        cols = [
            [None if g < s else [lane_of(part[b][g][0], at + j) for j in range(8)] for g in range(4)]
            for b in range(n)
        ]
        pivots = [None] * n
        for j in range(8):
            for b in range(n):
                here = cols[b][s]
                pivot = jnp.broadcast_to(here[j][j:j + 1, :], (8, 128))
                inverse = 1.0 / pivot
                pivots[b] = pivot if j == 0 else jnp.where(sub == j, pivot, pivots[b])
                if j == 7 and s == 3:
                    continue
                ratio = [
                    None if l <= j else jnp.broadcast_to(here[l][j:j + 1, :], (8, 128)) * inverse
                    for l in range(8)
                ]
                row = [jnp.broadcast_to(part[b][s][q][j:j + 1, :], (8, 128)) * inverse for q in lanes]
                for g in range(s, 4):
                    if g == s and j == 7:
                        continue
                    c = cols[b][g][j]
                    for l in range(j + 1, 8):
                        cols[b][g][l] = cols[b][g][l] - c * ratio[l]
                    if g == s:
                        c = jnp.where(sub > j, c, 0.0)
                    part[b][g] = [part[b][g][q] - c * row[q] for q in lanes]
        for b in range(n):
            scale = lax.rsqrt(pivots[b])
            part[b][s] = [v * scale for v in part[b][s]]
    return [jnp.concatenate([jnp.concatenate(v, axis=1) for v in p], axis=0) for p in part]


def factor(n, work, upper):
    for half in range(2):
        c0 = 128 * half
        for k in range(4):
            r0 = c0 + 32 * k
            rows = panel_step([work[b, r0:r0 + 32, c0:256] for b in range(n)], 32 * k, 256 - c0)
            for b in range(n):
                upper[b, r0:r0 + 32, c0:256] = rows[b]
            lo = r0 + 32
            if lo == 256:
                break
            for b in range(n):
                h, m, l = split3(rows[b])
                left = jnp.concatenate([h, h, m, h, m, l], axis=0)
                right = jnp.concatenate([h, m, h, l, m, h], axis=0)
                update = dot(left, right, TN)
                if half == 0:
                    if lo < 128:
                        work[b, lo:128, :] = work[b, lo:128, :] - update[lo:128, :]
                    work[b, 128:256, 128:256] = work[b, 128:256, 128:256] - update[128:256, 128:256]
                else:
                    work[b, lo:256, 128:256] = work[b, lo:256, 128:256] - update[lo - 128:128, :]


def factor_kernel(scales, slices_ref, nodes_ref, root_ref, work, upper):
    n = len(scales)
    ri = lax.broadcasted_iota(jnp.int32, (128, 128), 0)
    ci = lax.broadcasted_iota(jnp.int32, (128, 128), 1)
    eye = jnp.where(ri == ci, 1.0, 0.0)
    for b in range(n):
        t = jnp.concatenate([slices_ref[r, b] for r in range(8)], axis=0) * scales[b]
        work[b, 0:64, 0:128] = t[0:64] + eye[0:64]
        work[b, 0:64, 128:256] = t[64:128]
        work[b, 64:128, 0:128] = t[256:320] + eye[64:128]
        work[b, 64:128, 128:256] = t[128:192]
        work[b, 128:192, 128:256] = t[192:256] + eye[0:64]
        work[b, 192:256, 128:256] = pltpu.roll(t[256:320], 64, 1) + eye[64:128]
    factor(n, work, upper)
    below = ri >= ci
    for b in range(n):
        first = jnp.where(below, upper[b, 0:128, 0:128].T, 0.0)
        cross = upper[b, 0:128, 128:256].T
        second = jnp.where(below, upper[b, 128:256, 128:256].T, 0.0)
        low = jnp.concatenate(
            [
                jnp.concatenate([first, jnp.zeros((128, 128), F)], axis=1),
                jnp.concatenate([cross, second], axis=1),
            ],
            axis=0,
        )
        if b < LEVELS:
            nodes_ref[0, b] = low
        else:
            root_ref[...] = low


def factors(slices, scales):
    n = len(scales)
    return pl.pallas_call(
        functools.partial(factor_kernel, scales),
        out_shape=(
            jax.ShapeDtypeStruct((1, LEVELS, 256, 256), F),
            jax.ShapeDtypeStruct((256, 256), F),
        ),
        in_specs=[VM],
        out_specs=(VM, VM),
        scratch_shapes=[pltpu.VMEM((n, 256, 256), F)] * 2,
        compiler_params=pltpu.CompilerParams(vmem_limit_bytes=LIMIT),
    )(slices)


def line_kernel(base_ref, slices, level2, level3, line):
    z = base_ref[0] // (2 * BLOCKS) % 8
    two = z // 2 * 2
    four = z // 4 * 4
    level2[...] = slices[two] + slices[two + 1]
    level3[...] = (slices[four] + slices[four + 1]) + (slices[four + 2] + slices[four + 3])
    low = (slices[0] + slices[1]) + (slices[2] + slices[3])
    high = (slices[4] + slices[5]) + (slices[6] + slices[7])
    total = low + high
    for k in range(8):
        line[k] = total


def line_sums(base, slices):
    one = jax.ShapeDtypeStruct(slices.shape[1:], F)
    return pl.pallas_call(
        line_kernel,
        out_shape=(one, one, jax.ShapeDtypeStruct(slices.shape, F)),
        in_specs=[SM, VM],
        out_specs=(VM, VM, VM),
        compiler_params=pltpu.CompilerParams(vmem_limit_bytes=LIMIT),
    )(base, slices)


def exchange(x, axes):
    return lax.all_to_all(x, axes, 0, 0)


def to_all(x, axes, n):
    return exchange(jnp.broadcast_to(x[None], (n,) + x.shape), axes)


def body(points, probes, near_list, near_count):
    leaf = ("y", "z", "c")
    size = lax.axis_size(leaf)
    rows = points.shape[0]
    packed = jnp.concatenate([probes.T, points.T], axis=0)
    across = [(i, (i + (1 if i % 2 else -1)) % size) for i in range(size)]
    far = lax.ppermute(packed, leaf, across)
    near = lax.ppermute(packed, leaf, [(i, i ^ 1) for i in range(size)])
    base = (lax.axis_index(leaf) * BLOCKS).astype(jnp.int32).reshape(1)
    part, sides, ids, end = own_tiles(base, near_list, near_count, packed)
    turned, send = halo_tiles(ids, end, near, far, sides, part)
    samples = turned.T
    columns = exchange(send, "x")
    pieces = gram(columns).reshape(8, 40, 128)
    level1 = jnp.sum(exchange(pieces, ("c", "x")), axis=0)
    along_z = to_all(level1, "z", 8)
    level2, level3, line = line_sums(base, along_z)
    along_y = exchange(line, "y")
    root = jnp.sum(along_y, axis=0)
    slices = to_all(jnp.stack([level1, level2, level3, root]), ("c", "x"), 8)
    scales = [1.0 / (rows * 2 ** (l + 1)) for l in range(LEVELS)] + [1.0 / (rows * size)]
    node_factors, root_factor = factors(slices, scales)
    return samples, node_factors, root_factor


def solution(mesh):
    fine = Mesh(mesh.devices.reshape(8, 8, 2, 4), ("y", "z", "c", "x"))
    leaf = ("y", "z", "c")
    return jax.shard_map(
        body,
        mesh=fine,
        in_specs=(P(leaf, None), P(leaf, "x"), P(leaf, None), P(leaf)),
        out_specs=(P(leaf, "x"), P(leaf, None, None, None), P()),
        check_vma=False,
    )
```

```python
import functools

import jax
import jax.numpy as jnp
from jax import lax
from jax.experimental import pallas as pl
from jax.experimental.pallas import tpu as pltpu
from jax.sharding import Mesh, PartitionSpec as P

LEVELS = 3
BLOCKS = 8
BOX = 256
SLOTS = 16
GROUP = 8
ENTRIES = BLOCKS * SLOTS + 4 * GROUP
BF = jnp.bfloat16
F = jnp.float32
NN = (((1,), (0,)), ((), ()))
NT = (((1,), (1,)), ((), ()))
TN = (((0,), (0,)), ((), ()))
LOG2E_OVER_32 = 1.4426950408889634 / 32.0
LIMIT = 20 << 20
VM = pl.BlockSpec(memory_space=pltpu.VMEM)
SM = pl.BlockSpec(memory_space=pltpu.SMEM)


def dot(a, b, dims):
    return lax.dot_general(a, b, dims, preferred_element_type=F)


def split3(x):
    h = x.astype(BF)
    r = x - h.astype(F)
    m = r.astype(BF)
    return h, m, (r - m.astype(F)).astype(BF)


def squared(box):
    wide = box[64:128].astype(F)
    sq = jnp.sum(wide * wide, axis=0, keepdims=True)
    h = sq.astype(BF).astype(F)
    m = (sq - h).astype(BF).astype(F)
    return h, m, sq - h - m, lax.broadcasted_iota(jnp.int32, (16, BOX), 0)


def extended(head, points):
    return jnp.concatenate([head.astype(BF), jnp.zeros((48, BOX), BF), points], axis=0)


def other_side(box):
    h, m, l, row = squared(box)
    head = jnp.where(row == 0, h, jnp.where(row == 1, m, jnp.where(row == 2, l, jnp.where(row < 6, 1.0, 0.0))))
    return extended(head, box[64:128]).T


def own_side(box):
    h, m, l, row = squared(box)
    head = jnp.where(row < 3, -1.0, jnp.where(row == 3, -h, jnp.where(row == 4, -m, jnp.where(row == 5, -l, 0.0))))
    return extended(head, (box[64:128].astype(F) * 2.0).astype(BF))


def build_lists(base, list_ref, count_ref, own, halo):
    core = (base // BLOCKS) % 2

    def of_box(b, counts):
        def of_slot(s, counts):
            in_own, in_halo = counts
            j = list_ref[b, s] - base
            own[0, in_own] = b
            own[1, in_own] = j
            halo[0, in_halo] = b
            before = (j < 0).astype(jnp.int32)
            halo[1, in_halo] = jnp.where(j < 0, j + BLOCKS, j - BLOCKS) + BLOCKS * (before ^ core)
            inside = jnp.logical_and(j >= 0, j < BLOCKS).astype(jnp.int32)
            return in_own + inside, in_halo + 1 - inside

        return lax.fori_loop(0, count_ref[b], of_slot, counts)

    return lax.fori_loop(0, BLOCKS, of_box, (jnp.int32(GROUP), jnp.int32(GROUP)))


def run_list(end, ids, own, other, probes, parts, total):
    parts[...] = jnp.zeros_like(parts)

    def step(t, _):
        at = [t * GROUP + k for k in range(GROUP)]
        for k in range(GROUP):
            left = probes[ids[1, at[k] - GROUP]]
            i = ids[0, at[k] - GROUP]
            total[i] = total[i] + dot(jnp.concatenate([left, left], axis=1), parts[k], NN)
            tile = jnp.exp2(dot(other[ids[1, at[k]]], own[ids[0, at[k]]], NN) * LOG2E_OVER_32)
            h = tile.astype(BF)
            parts[k, 0:BOX] = h
            parts[k, BOX:2 * BOX] = (tile - h.astype(F)).astype(BF)
        return 0

    lax.fori_loop(1, (end + GROUP - 1) // GROUP + 1, step, 0)


def own_kernel(
    base_ref, list_hbm, count_hbm, own_ref, total, sides, halo_ids, halo_end,
    other, probes, parts, ids, list_ref, count_ref, sems,
):
    copies = [
        pltpu.make_async_copy(list_hbm, list_ref, sems.at[0]),
        pltpu.make_async_copy(count_hbm, count_ref, sems.at[1]),
    ]
    for copy in copies:
        copy.start()
    for b in range(BLOCKS):
        box = own_ref[:, BOX * b:BOX * b + BOX]
        other[b] = other_side(box)
        sides[b] = own_side(box)
        probes[b] = box[0:64]
    other[BLOCKS] = jnp.zeros((BOX, 128), BF)
    probes[BLOCKS] = jnp.zeros((64, BOX), BF)
    total[...] = jnp.zeros_like(total)
    for copy in copies:
        copy.wait()
    end, end_halo = build_lists(base_ref[0], list_ref, count_ref, ids, halo_ids)
    halo_end[0] = end_halo
    for k in range(GROUP):
        for start_ids, null, last in ((ids, BLOCKS, end), (halo_ids, 2 * BLOCKS, end_halo)):
            for e in (k, last + k, last + GROUP + k):
                start_ids[0, e] = 0
                start_ids[1, e] = null
    run_list(end, ids, sides, other, probes, parts, total)


def halo_kernel(ids, end_ref, near_ref, far_ref, sides, part, turned, send, other, probes, parts, total):
    for q, ref in enumerate((near_ref, far_ref)):
        for b in range(BLOCKS):
            box = ref[:, BOX * b:BOX * b + BOX]
            other[BLOCKS * q + b] = other_side(box)
            probes[BLOCKS * q + b] = box[0:64]
    other[2 * BLOCKS] = jnp.zeros((BOX, 128), BF)
    probes[2 * BLOCKS] = jnp.zeros((64, BOX), BF)
    total[...] = part[...]
    run_list(end_ref[0], ids, sides, other, probes, parts, total)
    for b in range(BLOCKS):
        turned[:, BOX * b:BOX * b + BOX] = total[b]
        send[b // 2, b % 2] = total[b]


def list_scratch(boxes):
    return [
        pltpu.VMEM((boxes + 1, BOX, 128), BF),
        pltpu.VMEM((boxes + 1, 64, BOX), BF),
        pltpu.VMEM((GROUP, 2 * BOX, BOX), BF),
    ]


def tiles_cost():
    return pl.CostEstimate(
        flops=64 * 3 * BOX * BOX * 128 * 2, bytes_accessed=4 << 20, transcendentals=64 * BOX * BOX
    )


def own_tiles(base, near_list, near_count, own):
    return pl.pallas_call(
        own_kernel,
        out_shape=(
            jax.ShapeDtypeStruct((BLOCKS, 64, BOX), F),
            jax.ShapeDtypeStruct((BLOCKS, 128, BOX), BF),
            jax.ShapeDtypeStruct((2, ENTRIES), jnp.int32),
            jax.ShapeDtypeStruct((1,), jnp.int32),
        ),
        in_specs=[SM, pl.BlockSpec(memory_space=pltpu.HBM), pl.BlockSpec(memory_space=pltpu.HBM), VM],
        out_specs=(VM, VM, SM, SM),
        scratch_shapes=list_scratch(BLOCKS)
        + [
            pltpu.SMEM((2, ENTRIES), jnp.int32),
            pltpu.SMEM((BLOCKS, SLOTS), jnp.int32),
            pltpu.SMEM((BLOCKS,), jnp.int32),
            pltpu.SemaphoreType.DMA((2,)),
        ],
        compiler_params=pltpu.CompilerParams(vmem_limit_bytes=LIMIT),
        cost_estimate=tiles_cost(),
    )(base, near_list, near_count, own)


def halo_tiles(ids, end, near, far, sides, part):
    return pl.pallas_call(
        halo_kernel,
        out_shape=(
            jax.ShapeDtypeStruct((64, BLOCKS * BOX), F),
            jax.ShapeDtypeStruct((BLOCKS // 2, 2, 64, BOX), F),
        ),
        in_specs=[SM, SM] + [VM] * 4,
        out_specs=(VM, VM),
        scratch_shapes=list_scratch(2 * BLOCKS) + [pltpu.VMEM((BLOCKS, 64, BOX), F)],
        compiler_params=pltpu.CompilerParams(vmem_limit_bytes=LIMIT),
        cost_estimate=tiles_cost(),
    )(ids, end, near, far, sides, part)


def gram_kernel(columns_ref, out_ref):
    g = None
    for b in range(2):
        h, m, l = split3(jnp.concatenate([columns_ref[q, b] for q in range(4)], axis=0))
        left = jnp.concatenate([h, h, m, h, m, l], axis=1)
        right = jnp.concatenate([h, m, h, l, m, h], axis=1)
        term = dot(left, right, NT)
        g = term if g is None else g + term
    out_ref[0:64, :] = g[0:64, 0:128]
    out_ref[64:128, :] = g[0:64, 128:256]
    out_ref[128:192, :] = g[64:128, 128:256]
    out_ref[192:256, :] = g[128:192, 128:256]
    low_lanes = lax.broadcasted_iota(jnp.int32, (64, 128), 1) < 64
    out_ref[256:320, :] = jnp.where(low_lanes, pltpu.roll(g[192:256, 128:256], 64, 1), g[64:128, 0:128])


def gram(columns):
    return pl.pallas_call(
        gram_kernel,
        out_shape=jax.ShapeDtypeStruct((320, 128), F),
        in_specs=[VM],
        out_specs=VM,
        compiler_params=pltpu.CompilerParams(vmem_limit_bytes=LIMIT),
    )(columns)


def lane_of(x, lane):
    index = jnp.full((8, 128, 1), lane, jnp.int32)
    dims = lax.GatherDimensionNumbers(
        offset_dims=(),
        collapsed_slice_dims=(1,),
        start_index_map=(1,),
        operand_batching_dims=(0,),
        start_indices_batching_dims=(0,),
    )
    return lax.gather(x, index, dims, (1, 1), mode=lax.GatherScatterMode.PROMISE_IN_BOUNDS)


def panel_step(rows, off, width):
    n = len(rows)
    lanes = range(width // 128)
    sub = lax.broadcasted_iota(jnp.int32, (8, 128), 0)
    part = [[[r[8 * g:8 * g + 8, 128 * q:128 * q + 128] for q in lanes] for g in range(4)] for r in rows]
    for s in range(4):
        at = off + 8 * s
        cols = [
            [None if g < s else [lane_of(part[b][g][0], at + j) for j in range(8)] for g in range(4)]
            for b in range(n)
        ]
        pivots = [None] * n
        for j in range(8):
            for b in range(n):
                here = cols[b][s]
                pivot = jnp.broadcast_to(here[j][j:j + 1, :], (8, 128))
                inverse = 1.0 / pivot
                pivots[b] = pivot if j == 0 else jnp.where(sub == j, pivot, pivots[b])
                if j == 7 and s == 3:
                    continue
                ratio = [
                    None if l <= j else jnp.broadcast_to(here[l][j:j + 1, :], (8, 128)) * inverse
                    for l in range(8)
                ]
                row = [jnp.broadcast_to(part[b][s][q][j:j + 1, :], (8, 128)) * inverse for q in lanes]
                for g in range(s, 4):
                    if g == s and j == 7:
                        continue
                    c = cols[b][g][j]
                    for l in range(j + 1, 8):
                        cols[b][g][l] = cols[b][g][l] - c * ratio[l]
                    if g == s:
                        c = jnp.where(sub > j, c, 0.0)
                    part[b][g] = [part[b][g][q] - c * row[q] for q in lanes]
        for b in range(n):
            scale = lax.rsqrt(pivots[b])
            part[b][s] = [v * scale for v in part[b][s]]
    return [jnp.concatenate([jnp.concatenate(v, axis=1) for v in p], axis=0) for p in part]


def products(rows, lanes):
    h, m, l = split3(rows)
    left = jnp.concatenate([h, h, m, h, m, l], axis=0)[:, :lanes]
    return dot(left, jnp.concatenate([h, m, h, l, m, h], axis=0), TN)


def factor(n, work, upper):
    for c0 in (0, 128):
        for k in range(4):
            r0 = c0 + 32 * k
            rows = panel_step([work[b, r0:r0 + 32, c0:256] for b in range(n)], 32 * k, 256 - c0)
            for b in range(n):
                upper[b, r0:r0 + 32, c0:256] = rows[b]
            lo = r0 + 32
            for b in range(n):
                if k < 3:
                    update = products(rows[b], 128)
                    work[b, lo:c0 + 128, c0:256] = work[b, lo:c0 + 128, c0:256] - update[lo - c0:, :]
                elif c0 == 0:
                    update = products(upper[b, 0:128, 128:256], 128)
                    work[b, 128:256, 128:256] = work[b, 128:256, 128:256] - update


def factor_kernel(scales, slices_ref, nodes_ref, root_ref, work, upper):
    n = len(scales)
    ri = lax.broadcasted_iota(jnp.int32, (128, 128), 0)
    ci = lax.broadcasted_iota(jnp.int32, (128, 128), 1)
    eye = jnp.where(ri == ci, 1.0, 0.0)
    for b in range(n):
        t = jnp.concatenate([slices_ref[r, b] for r in range(8)], axis=0) * scales[b]
        work[b, 0:64, 0:128] = t[0:64] + eye[0:64]
        work[b, 0:64, 128:256] = t[64:128]
        work[b, 64:128, 0:128] = t[256:320] + eye[64:128]
        work[b, 64:128, 128:256] = t[128:192]
        work[b, 128:192, 128:256] = t[192:256] + eye[0:64]
        work[b, 192:256, 128:256] = pltpu.roll(t[256:320], 64, 1) + eye[64:128]
    factor(n, work, upper)
    below = ri >= ci
    for b in range(n):
        first = jnp.where(below, upper[b, 0:128, 0:128].T, 0.0)
        cross = upper[b, 0:128, 128:256].T
        second = jnp.where(below, upper[b, 128:256, 128:256].T, 0.0)
        low = jnp.concatenate(
            [
                jnp.concatenate([first, jnp.zeros((128, 128), F)], axis=1),
                jnp.concatenate([cross, second], axis=1),
            ],
            axis=0,
        )
        if b < LEVELS:
            nodes_ref[0, b] = low
        else:
            root_ref[...] = low


def factors(slices, scales):
    n = len(scales)
    return pl.pallas_call(
        functools.partial(factor_kernel, scales),
        out_shape=(
            jax.ShapeDtypeStruct((1, LEVELS, 256, 256), F),
            jax.ShapeDtypeStruct((256, 256), F),
        ),
        in_specs=[VM],
        out_specs=(VM, VM),
        scratch_shapes=[pltpu.VMEM((n, 256, 256), F)] * 2,
        compiler_params=pltpu.CompilerParams(vmem_limit_bytes=LIMIT),
    )(slices)


def line_kernel(base_ref, slices, level2, level3, line):
    z = base_ref[0] // (2 * BLOCKS) % 8
    two = z // 2 * 2
    four = z // 4 * 4
    level2[...] = slices[two] + slices[two + 1]
    level3[...] = (slices[four] + slices[four + 1]) + (slices[four + 2] + slices[four + 3])
    low = (slices[0] + slices[1]) + (slices[2] + slices[3])
    high = (slices[4] + slices[5]) + (slices[6] + slices[7])
    total = low + high
    for k in range(8):
        line[k] = total


def line_sums(base, slices):
    one = jax.ShapeDtypeStruct(slices.shape[1:], F)
    return pl.pallas_call(
        line_kernel,
        out_shape=(one, one, jax.ShapeDtypeStruct(slices.shape, F)),
        in_specs=[SM, VM],
        out_specs=(VM, VM, VM),
        compiler_params=pltpu.CompilerParams(vmem_limit_bytes=LIMIT),
    )(base, slices)


def exchange(x, axes):
    return lax.all_to_all(x, axes, 0, 0)


def to_all(x, axes, n):
    return exchange(jnp.broadcast_to(x[None], (n,) + x.shape), axes)


def body(points, probes, near_list, near_count):
    leaf = ("y", "z", "c")
    size = lax.axis_size(leaf)
    rows = points.shape[0]
    packed = jnp.concatenate([probes.T, points.T], axis=0)
    across = [(i, (i + (1 if i % 2 else -1)) % size) for i in range(size)]
    far = lax.ppermute(packed, leaf, across)
    near = lax.ppermute(packed, leaf, [(i, i ^ 1) for i in range(size)])
    base = (lax.axis_index(leaf) * BLOCKS).astype(jnp.int32).reshape(1)
    part, sides, ids, end = own_tiles(base, near_list, near_count, packed)
    turned, send = halo_tiles(ids, end, near, far, sides, part)
    samples = turned.T
    columns = exchange(send, "x")
    pieces = gram(columns).reshape(8, 40, 128)
    level1 = jnp.sum(exchange(pieces, ("c", "x")), axis=0)
    along_z = to_all(level1, "z", 8)
    level2, level3, line = line_sums(base, along_z)
    along_y = exchange(line, "y")
    root = jnp.sum(along_y, axis=0)
    slices = to_all(jnp.stack([level1, level2, level3, root]), ("c", "x"), 8)
    scales = [1.0 / (rows * 2 ** (l + 1)) for l in range(LEVELS)] + [1.0 / (rows * size)]
    node_factors, root_factor = factors(slices, scales)
    return samples, node_factors, root_factor


def solution(mesh):
    fine = Mesh(mesh.devices.reshape(8, 8, 2, 4), ("y", "z", "c", "x"))
    leaf = ("y", "z", "c")
    return jax.shard_map(
        body,
        mesh=fine,
        in_specs=(P(leaf, None), P(leaf, "x"), P(leaf, None), P(leaf)),
        out_specs=(P(leaf, "x"), P(leaf, None, None, None), P()),
        check_vma=False,
    )
```

```python
import functools

import jax
import jax.numpy as jnp
from jax import lax
from jax.experimental import pallas as pl
from jax.experimental.pallas import tpu as pltpu
from jax.sharding import Mesh, PartitionSpec as P

LEVELS = 3
BLOCKS = 8
BOX = 256
SLOTS = 16
GROUP = 8
ENTRIES = BLOCKS * SLOTS + 3 * GROUP
BF = jnp.bfloat16
F = jnp.float32
NN = (((1,), (0,)), ((), ()))
NT = (((1,), (1,)), ((), ()))
TN = (((0,), (0,)), ((), ()))
LOG2E_OVER_32 = 1.4426950408889634 / 32.0
LIMIT = 20 << 20
VM = pl.BlockSpec(memory_space=pltpu.VMEM)
SM = pl.BlockSpec(memory_space=pltpu.SMEM)


def dot(a, b, dims):
    return lax.dot_general(a, b, dims, preferred_element_type=F)


def split3(x):
    h = x.astype(BF)
    r = x - h.astype(F)
    m = r.astype(BF)
    return h, m, (r - m.astype(F)).astype(BF)


def squared(box):
    wide = box[64:128].astype(F)
    sq = jnp.sum(wide * wide, axis=0, keepdims=True)
    h = sq.astype(BF).astype(F)
    m = (sq - h).astype(BF).astype(F)
    return h, m, sq - h - m, lax.broadcasted_iota(jnp.int32, (16, BOX), 0)


def extended(head, points):
    return jnp.concatenate([head.astype(BF), jnp.zeros((48, BOX), BF), points], axis=0)


def other_side(box):
    h, m, l, row = squared(box)
    head = jnp.where(row == 0, h, jnp.where(row == 1, m, jnp.where(row == 2, l, jnp.where(row < 6, 1.0, 0.0))))
    return extended(head, box[64:128]).T


def own_side(box):
    h, m, l, row = squared(box)
    head = jnp.where(row < 3, -1.0, jnp.where(row == 3, -h, jnp.where(row == 4, -m, jnp.where(row == 5, -l, 0.0))))
    return extended(head, (box[64:128].astype(F) * 2.0).astype(BF))


def build_lists(base, list_ref, count_ref, own, halo):
    core = (base // BLOCKS) % 2

    def of_box(b, counts):
        def of_slot(s, counts):
            in_own, in_halo = counts
            j = list_ref[b, s] - base
            own[0, in_own] = b
            own[1, in_own] = j
            halo[0, in_halo] = b
            before = (j < 0).astype(jnp.int32)
            halo[1, in_halo] = jnp.where(j < 0, j + BLOCKS, j - BLOCKS) + BLOCKS * (before ^ core)
            inside = jnp.logical_and(j >= 0, j < BLOCKS).astype(jnp.int32)
            return in_own + inside, in_halo + 1 - inside

        return lax.fori_loop(0, count_ref[b], of_slot, counts)

    return lax.fori_loop(0, BLOCKS, of_box, (jnp.int32(GROUP), jnp.int32(GROUP)))


def run_list(end, ids, own, other, probes, parts, total):
    def make(t, k):
        e = t * GROUP + k
        tile = jnp.exp2(dot(other[ids[1, e]], own[ids[0, e]], NN) * LOG2E_OVER_32)
        h = tile.astype(BF)
        parts[k, 0:BOX] = h
        parts[k, BOX:2 * BOX] = (tile - h.astype(F)).astype(BF)

    def use(t, k):
        e = t * GROUP + k
        left = probes[ids[1, e]]
        i = ids[0, e]
        total[i] = total[i] + dot(jnp.concatenate([left, left], axis=1), parts[k], NN)

    def step(t, _):
        for k in range(GROUP):
            use(t - 1, k)
            make(t, k)
        return 0

    last = jnp.maximum((end - 1) // GROUP, 1)
    for k in range(GROUP):
        make(1, k)
    lax.fori_loop(2, last + 1, step, 0)
    for k in range(GROUP):
        use(last, k)


def own_kernel(
    base_ref, list_hbm, count_hbm, own_ref, total, sides, halo_ids, halo_end,
    other, probes, parts, ids, list_ref, count_ref, sems,
):
    copies = [
        pltpu.make_async_copy(list_hbm, list_ref, sems.at[0]),
        pltpu.make_async_copy(count_hbm, count_ref, sems.at[1]),
    ]
    for copy in copies:
        copy.start()
    for b in range(BLOCKS):
        box = own_ref[:, BOX * b:BOX * b + BOX]
        other[b] = other_side(box)
        sides[b] = own_side(box)
        probes[b] = box[0:64]
    other[BLOCKS] = jnp.zeros((BOX, 128), BF)
    probes[BLOCKS] = jnp.zeros((64, BOX), BF)
    total[...] = jnp.zeros_like(total)
    for copy in copies:
        copy.wait()
    end, end_halo = build_lists(base_ref[0], list_ref, count_ref, ids, halo_ids)
    halo_end[0] = end_halo
    for k in range(GROUP):
        for to, null, last in ((ids, BLOCKS, end), (halo_ids, 2 * BLOCKS, end_halo)):
            to[0, last + k] = 0
            to[1, last + k] = null
    run_list(end, ids, sides, other, probes, parts, total)


def halo_kernel(ids, end_ref, near_ref, far_ref, sides, part, send, other, probes, parts, total):
    for q, ref in enumerate((near_ref, far_ref)):
        for b in range(BLOCKS):
            box = ref[:, BOX * b:BOX * b + BOX]
            other[BLOCKS * q + b] = other_side(box)
            probes[BLOCKS * q + b] = box[0:64]
    other[2 * BLOCKS] = jnp.zeros((BOX, 128), BF)
    probes[2 * BLOCKS] = jnp.zeros((64, BOX), BF)
    total[...] = part[...]
    run_list(end_ref[0], ids, sides, other, probes, parts, total)
    for b in range(BLOCKS):
        send[b // 2, b % 2] = total[b]


def list_scratch(boxes):
    return [
        pltpu.VMEM((boxes + 1, BOX, 128), BF),
        pltpu.VMEM((boxes + 1, 64, BOX), BF),
        pltpu.VMEM((GROUP, 2 * BOX, BOX), BF),
    ]


def tiles_cost():
    return pl.CostEstimate(
        flops=64 * 3 * BOX * BOX * 128 * 2, bytes_accessed=4 << 20, transcendentals=64 * BOX * BOX
    )


def own_tiles(base, near_list, near_count, own):
    return pl.pallas_call(
        own_kernel,
        out_shape=(
            jax.ShapeDtypeStruct((BLOCKS, 64, BOX), F),
            jax.ShapeDtypeStruct((BLOCKS, 128, BOX), BF),
            jax.ShapeDtypeStruct((2, ENTRIES), jnp.int32),
            jax.ShapeDtypeStruct((1,), jnp.int32),
        ),
        in_specs=[SM, pl.BlockSpec(memory_space=pltpu.HBM), pl.BlockSpec(memory_space=pltpu.HBM), VM],
        out_specs=(VM, VM, SM, SM),
        scratch_shapes=list_scratch(BLOCKS)
        + [
            pltpu.SMEM((2, ENTRIES), jnp.int32),
            pltpu.SMEM((BLOCKS, SLOTS), jnp.int32),
            pltpu.SMEM((BLOCKS,), jnp.int32),
            pltpu.SemaphoreType.DMA((2,)),
        ],
        compiler_params=pltpu.CompilerParams(vmem_limit_bytes=LIMIT),
        cost_estimate=tiles_cost(),
    )(base, near_list, near_count, own)


def halo_tiles(ids, end, near, far, sides, part):
    return pl.pallas_call(
        halo_kernel,
        out_shape=jax.ShapeDtypeStruct((BLOCKS // 2, 2, 64, BOX), F),
        in_specs=[SM, SM] + [VM] * 4,
        out_specs=VM,
        scratch_shapes=list_scratch(2 * BLOCKS) + [pltpu.VMEM((BLOCKS, 64, BOX), F)],
        compiler_params=pltpu.CompilerParams(vmem_limit_bytes=LIMIT),
        cost_estimate=tiles_cost(),
    )(ids, end, near, far, sides, part)


def gram_kernel(columns_ref, out_ref):
    g = None
    for b in range(2):
        h, m, l = split3(jnp.concatenate([columns_ref[q, b] for q in range(4)], axis=0))
        left = jnp.concatenate([h, h, m, h, m, l], axis=1)
        right = jnp.concatenate([h, m, h, l, m, h], axis=1)
        term = dot(left, right, NT)
        g = term if g is None else g + term
    out_ref[0:64, :] = g[0:64, 0:128]
    out_ref[64:128, :] = g[0:64, 128:256]
    out_ref[128:192, :] = g[64:128, 128:256]
    out_ref[192:256, :] = g[128:192, 128:256]
    low_lanes = lax.broadcasted_iota(jnp.int32, (64, 128), 1) < 64
    out_ref[256:320, :] = jnp.where(low_lanes, pltpu.roll(g[192:256, 128:256], 64, 1), g[64:128, 0:128])


def gram(columns):
    return pl.pallas_call(
        gram_kernel,
        out_shape=jax.ShapeDtypeStruct((320, 128), F),
        in_specs=[VM],
        out_specs=VM,
        compiler_params=pltpu.CompilerParams(vmem_limit_bytes=LIMIT),
    )(columns)


def lane_of(x, lane):
    index = jnp.full((8, 128, 1), lane, jnp.int32)
    dims = lax.GatherDimensionNumbers(
        offset_dims=(),
        collapsed_slice_dims=(1,),
        start_index_map=(1,),
        operand_batching_dims=(0,),
        start_indices_batching_dims=(0,),
    )
    return lax.gather(x, index, dims, (1, 1), mode=lax.GatherScatterMode.PROMISE_IN_BOUNDS)


def panel_step(rows, off, width):
    n = len(rows)
    lanes = range(width // 128)
    sub = lax.broadcasted_iota(jnp.int32, (8, 128), 0)
    part = [[[r[8 * g:8 * g + 8, 128 * q:128 * q + 128] for q in lanes] for g in range(4)] for r in rows]
    for s in range(4):
        at = off + 8 * s
        cols = [
            [None if g < s else [lane_of(part[b][g][0], at + j) for j in range(8)] for g in range(4)]
            for b in range(n)
        ]
        pivots = [None] * n
        for j in range(8):
            for b in range(n):
                here = cols[b][s]
                pivot = jnp.broadcast_to(here[j][j:j + 1, :], (8, 128))
                inverse = 1.0 / pivot
                pivots[b] = pivot if j == 0 else jnp.where(sub == j, pivot, pivots[b])
                if j == 7 and s == 3:
                    continue
                ratio = [
                    None if l <= j else jnp.broadcast_to(here[l][j:j + 1, :], (8, 128)) * inverse
                    for l in range(8)
                ]
                row = [jnp.broadcast_to(part[b][s][q][j:j + 1, :], (8, 128)) * inverse for q in lanes]
                for g in range(s, 4):
                    if g == s and j == 7:
                        continue
                    c = cols[b][g][j]
                    for l in range(j + 1, 8):
                        cols[b][g][l] = cols[b][g][l] - c * ratio[l]
                    if g == s:
                        c = jnp.where(sub > j, c, 0.0)
                    part[b][g] = [part[b][g][q] - c * row[q] for q in lanes]
        for b in range(n):
            scale = lax.rsqrt(pivots[b])
            part[b][s] = [v * scale for v in part[b][s]]
    return [jnp.concatenate([jnp.concatenate(v, axis=1) for v in p], axis=0) for p in part]


def products(rows, lanes):
    h, m, l = split3(rows)
    left = jnp.concatenate([h, h, m, h, m, l], axis=0)[:, :lanes]
    return dot(left, jnp.concatenate([h, m, h, l, m, h], axis=0), TN)


def factor(n, work, upper, beside):
    for c0 in (0, 128):
        for k in range(4):
            r0 = c0 + 32 * k
            rows = panel_step([work[b, r0:r0 + 32, c0:256] for b in range(n)], 32 * k, 256 - c0)
            for b in range(n):
                upper[b, r0:r0 + 32, c0:256] = rows[b]
            lo = r0 + 32
            for b in range(n):
                if k < 3:
                    update = products(rows[b], 128)
                    work[b, lo:c0 + 128, c0:256] = work[b, lo:c0 + 128, c0:256] - update[lo - c0:, :]
                elif c0 == 0:
                    update = products(upper[b, 0:128, 128:256], 128)
                    work[b, 128:256, 128:256] = work[b, 128:256, 128:256] - update
            if c0:
                beside(k)


def factor_kernel(scales, slices_ref, send_ref, turned, nodes, root, work, upper, left, right, sems):
    n = len(scales)
    copies = []

    def copy(src, dst):
        copies.append(pltpu.make_async_copy(src, dst, sems.at[len(copies)]))
        copies[-1].start()

    for b in range(BLOCKS):
        copy(send_ref.at[b // 2, b % 2], turned.at[:, pl.ds(BOX * b, BOX)])
    ri = lax.broadcasted_iota(jnp.int32, (128, 128), 0)
    ci = lax.broadcasted_iota(jnp.int32, (128, 128), 1)
    eye = jnp.where(ri == ci, 1.0, 0.0)
    below = ri >= ci
    for b in range(n):
        t = jnp.concatenate([slices_ref[r, b] for r in range(8)], axis=0) * scales[b]
        work[b, 0:64, 0:128] = t[0:64] + eye[0:64]
        work[b, 0:64, 128:256] = t[64:128]
        work[b, 64:128, 0:128] = t[256:320] + eye[64:128]
        work[b, 64:128, 128:256] = t[128:192]
        work[b, 128:192, 128:256] = t[192:256] + eye[0:64]
        work[b, 192:256, 128:256] = pltpu.roll(t[256:320], 64, 1) + eye[64:128]

    def place(b, half):
        columns = pl.ds(128 * half, 128)
        return nodes.at[0, b, :, columns] if b < LEVELS else root.at[:, columns]

    def beside(k):
        for b in range(n):
            if k == b // 2:
                left[b, 0:128] = jnp.where(below, upper[b, 0:128, 0:128].T, 0.0)
                left[b, 128:256] = upper[b, 0:128, 128:256].T
                copy(left.at[b], place(b, 0))
            if k == 3:
                right[b, 0:128] = jnp.zeros((128, 128), F)
                right[b, 128:256] = jnp.where(below, upper[b, 128:256, 128:256].T, 0.0)
                copy(right.at[b], place(b, 1))

    factor(n, work, upper, beside)
    for c in copies:
        c.wait()


def factors(slices, send, scales):
    n = len(scales)
    any_place = pl.BlockSpec(memory_space=pl.ANY)
    return pl.pallas_call(
        functools.partial(factor_kernel, scales),
        out_shape=(
            jax.ShapeDtypeStruct((64, BLOCKS * BOX), F),
            jax.ShapeDtypeStruct((1, LEVELS, 256, 256), F),
            jax.ShapeDtypeStruct((256, 256), F),
        ),
        in_specs=[VM, VM],
        out_specs=(any_place,) * 3,
        scratch_shapes=[pltpu.VMEM((n, 256, 256), F)] * 2
        + [pltpu.VMEM((n, 256, 128), F)] * 2
        + [pltpu.SemaphoreType.DMA((BLOCKS + 2 * n,))],
        compiler_params=pltpu.CompilerParams(vmem_limit_bytes=LIMIT),
    )(slices, send)


def line_kernel(base_ref, slices, level2, level3, line):
    z = base_ref[0] // (2 * BLOCKS) % 8
    two = z // 2 * 2
    four = z // 4 * 4
    level2[...] = slices[two] + slices[two + 1]
    level3[...] = (slices[four] + slices[four + 1]) + (slices[four + 2] + slices[four + 3])
    low = (slices[0] + slices[1]) + (slices[2] + slices[3])
    high = (slices[4] + slices[5]) + (slices[6] + slices[7])
    total = low + high
    for k in range(8):
        line[k] = total


def line_sums(base, slices):
    one = jax.ShapeDtypeStruct(slices.shape[1:], F)
    return pl.pallas_call(
        line_kernel,
        out_shape=(one, one, jax.ShapeDtypeStruct(slices.shape, F)),
        in_specs=[SM, VM],
        out_specs=(VM, VM, VM),
        compiler_params=pltpu.CompilerParams(vmem_limit_bytes=LIMIT),
    )(base, slices)


def exchange(x, axes):
    return lax.all_to_all(x, axes, 0, 0)


def to_all(x, axes, n):
    return exchange(jnp.broadcast_to(x[None], (n,) + x.shape), axes)


def body(points, probes, near_list, near_count):
    leaf = ("y", "z", "c")
    size = lax.axis_size(leaf)
    rows = points.shape[0]
    packed = jnp.concatenate([probes.T, points.T], axis=0)
    across = [(i, (i + (1 if i % 2 else -1)) % size) for i in range(size)]
    far = lax.ppermute(packed, leaf, across)
    near = lax.ppermute(packed, leaf, [(i, i ^ 1) for i in range(size)])
    base = (lax.axis_index(leaf) * BLOCKS).astype(jnp.int32).reshape(1)
    part, sides, ids, end = own_tiles(base, near_list, near_count, packed)
    send = halo_tiles(ids, end, near, far, sides, part)
    columns = exchange(send, "x")
    pieces = gram(columns).reshape(8, 40, 128)
    level1 = jnp.sum(exchange(pieces, ("c", "x")), axis=0)
    along_z = to_all(level1, "z", 8)
    level2, level3, line = line_sums(base, along_z)
    along_y = exchange(line, "y")
    root = jnp.sum(along_y, axis=0)
    slices = to_all(jnp.stack([level1, level2, level3, root]), ("c", "x"), 8)
    scales = [1.0 / (rows * 2 ** (l + 1)) for l in range(LEVELS)] + [1.0 / (rows * size)]
    turned, node_factors, root_factor = factors(slices, send, scales)
    return turned.T, node_factors, root_factor


def solution(mesh):
    fine = Mesh(mesh.devices.reshape(8, 8, 2, 4), ("y", "z", "c", "x"))
    leaf = ("y", "z", "c")
    return jax.shard_map(
        body,
        mesh=fine,
        in_specs=(P(leaf, None), P(leaf, "x"), P(leaf, None), P(leaf)),
        out_specs=(P(leaf, "x"), P(leaf, None, None, None), P()),
        check_vma=False,
    )
```

```python
import functools

import jax
import jax.numpy as jnp
from jax import lax
from jax.experimental import pallas as pl
from jax.experimental.pallas import tpu as pltpu
from jax.sharding import Mesh, PartitionSpec as P

LEVELS = 3
BLOCKS = 8
BOX = 256
SLOTS = 16
GROUP = 8
ENTRIES = BLOCKS * SLOTS + 3 * GROUP
BF = jnp.bfloat16
F = jnp.float32
NN = (((1,), (0,)), ((), ()))
NT = (((1,), (1,)), ((), ()))
TN = (((0,), (0,)), ((), ()))
LOG2E_OVER_32 = 1.4426950408889634 / 32.0
LIMIT = 20 << 20
VM = pl.BlockSpec(memory_space=pltpu.VMEM)
SM = pl.BlockSpec(memory_space=pltpu.SMEM)


def dot(a, b, dims):
    return lax.dot_general(a, b, dims, preferred_element_type=F)


def split3(x):
    h = x.astype(BF)
    r = x - h.astype(F)
    m = r.astype(BF)
    return h, m, (r - m.astype(F)).astype(BF)


def squared(box):
    wide = box[64:128].astype(F)
    sq = jnp.sum(wide * wide, axis=0, keepdims=True)
    h = sq.astype(BF).astype(F)
    m = (sq - h).astype(BF).astype(F)
    return h, m, sq - h - m, lax.broadcasted_iota(jnp.int32, (16, BOX), 0)


def extended(head, points):
    return jnp.concatenate([head.astype(BF), jnp.zeros((48, BOX), BF), points], axis=0)


def other_side(box):
    h, m, l, row = squared(box)
    head = jnp.where(row == 0, h, jnp.where(row == 1, m, jnp.where(row == 2, l, jnp.where(row < 6, 1.0, 0.0))))
    return extended(head, box[64:128]).T


def own_side(box):
    h, m, l, row = squared(box)
    head = jnp.where(row < 3, -1.0, jnp.where(row == 3, -h, jnp.where(row == 4, -m, jnp.where(row == 5, -l, 0.0))))
    return extended(head, (box[64:128].astype(F) * 2.0).astype(BF))


def build_lists(base, list_ref, count_ref, own, halo):
    core = (base // BLOCKS) % 2

    def of_box(b, counts):
        def of_slot(s, counts):
            in_own, in_halo = counts
            j = list_ref[b, s] - base
            own[0, in_own] = b
            own[1, in_own] = j
            halo[0, in_halo] = b
            before = (j < 0).astype(jnp.int32)
            halo[1, in_halo] = jnp.where(j < 0, j + BLOCKS, j - BLOCKS) + BLOCKS * (before ^ core)
            inside = jnp.logical_and(j >= 0, j < BLOCKS).astype(jnp.int32)
            return in_own + inside, in_halo + 1 - inside

        return lax.fori_loop(0, count_ref[b], of_slot, counts)

    return lax.fori_loop(0, BLOCKS, of_box, (jnp.int32(GROUP), jnp.int32(GROUP)))


def run_list(end, ids, own, other, probes, parts, total):
    def make(t, k):
        e = t * GROUP + k
        tile = jnp.exp2(dot(other[ids[1, e]], own[ids[0, e]], NN) * LOG2E_OVER_32)
        h = tile.astype(BF)
        parts[k, 0:BOX] = h
        parts[k, BOX:2 * BOX] = (tile - h.astype(F)).astype(BF)

    def use(t, k):
        e = t * GROUP + k
        left = probes[ids[1, e]]
        i = ids[0, e]
        total[i] = total[i] + dot(jnp.concatenate([left, left], axis=1), parts[k], NN)

    def step(t, _):
        for k in range(GROUP):
            use(t - 1, k)
            make(t, k)
        return 0

    last = jnp.maximum((end - 1) // GROUP, 1)
    for k in range(GROUP):
        make(1, k)
    lax.fori_loop(2, last + 1, step, 0)
    for k in range(GROUP):
        use(last, k)


def own_kernel(
    base_ref, list_hbm, count_hbm, own_ref, total, sides, halo_ids, halo_end,
    other, probes, parts, ids, list_ref, count_ref, sems,
):
    copies = [
        pltpu.make_async_copy(list_hbm, list_ref, sems.at[0]),
        pltpu.make_async_copy(count_hbm, count_ref, sems.at[1]),
    ]
    for copy in copies:
        copy.start()
    for b in range(BLOCKS):
        box = own_ref[:, BOX * b:BOX * b + BOX]
        other[b] = other_side(box)
        sides[b] = own_side(box)
        probes[b] = box[0:64]
    other[BLOCKS] = jnp.zeros((BOX, 128), BF)
    probes[BLOCKS] = jnp.zeros((64, BOX), BF)
    total[...] = jnp.zeros_like(total)
    for copy in copies:
        copy.wait()
    end, end_halo = build_lists(base_ref[0], list_ref, count_ref, ids, halo_ids)
    halo_end[0] = end_halo
    for k in range(GROUP):
        for to, null, last in ((ids, BLOCKS, end), (halo_ids, 2 * BLOCKS, end_halo)):
            to[0, last + k] = 0
            to[1, last + k] = null
    run_list(end, ids, sides, other, probes, parts, total)


def halo_kernel(ids, end_ref, near_ref, far_ref, sides, part, send, other, probes, parts, total):
    for q, ref in enumerate((near_ref, far_ref)):
        for b in range(BLOCKS):
            box = ref[:, BOX * b:BOX * b + BOX]
            other[BLOCKS * q + b] = other_side(box)
            probes[BLOCKS * q + b] = box[0:64]
    other[2 * BLOCKS] = jnp.zeros((BOX, 128), BF)
    probes[2 * BLOCKS] = jnp.zeros((64, BOX), BF)
    total[...] = part[...]
    run_list(end_ref[0], ids, sides, other, probes, parts, total)
    for b in range(BLOCKS):
        send[b // 2, b % 2] = total[b]


def list_scratch(boxes):
    return [
        pltpu.VMEM((boxes + 1, BOX, 128), BF),
        pltpu.VMEM((boxes + 1, 64, BOX), BF),
        pltpu.VMEM((GROUP, 2 * BOX, BOX), BF),
    ]


def tiles_cost():
    return pl.CostEstimate(
        flops=64 * 3 * BOX * BOX * 128 * 2, bytes_accessed=4 << 20, transcendentals=64 * BOX * BOX
    )


def own_tiles(base, near_list, near_count, own):
    return pl.pallas_call(
        own_kernel,
        out_shape=(
            jax.ShapeDtypeStruct((BLOCKS, 64, BOX), F),
            jax.ShapeDtypeStruct((BLOCKS, 128, BOX), BF),
            jax.ShapeDtypeStruct((2, ENTRIES), jnp.int32),
            jax.ShapeDtypeStruct((1,), jnp.int32),
        ),
        in_specs=[SM, pl.BlockSpec(memory_space=pltpu.HBM), pl.BlockSpec(memory_space=pltpu.HBM), VM],
        out_specs=(VM, VM, SM, SM),
        scratch_shapes=list_scratch(BLOCKS)
        + [
            pltpu.SMEM((2, ENTRIES), jnp.int32),
            pltpu.SMEM((BLOCKS, SLOTS), jnp.int32),
            pltpu.SMEM((BLOCKS,), jnp.int32),
            pltpu.SemaphoreType.DMA((2,)),
        ],
        compiler_params=pltpu.CompilerParams(vmem_limit_bytes=LIMIT),
        cost_estimate=tiles_cost(),
    )(base, near_list, near_count, own)


def halo_tiles(ids, end, near, far, sides, part):
    return pl.pallas_call(
        halo_kernel,
        out_shape=jax.ShapeDtypeStruct((BLOCKS // 2, 2, 64, BOX), F),
        in_specs=[SM, SM] + [VM] * 4,
        out_specs=VM,
        scratch_shapes=list_scratch(2 * BLOCKS) + [pltpu.VMEM((BLOCKS, 64, BOX), F)],
        compiler_params=pltpu.CompilerParams(vmem_limit_bytes=LIMIT),
        cost_estimate=tiles_cost(),
    )(ids, end, near, far, sides, part)


def gram_kernel(columns_ref, out_ref):
    g = None
    for b in range(2):
        h, m, l = split3(jnp.concatenate([columns_ref[q, b] for q in range(4)], axis=0))
        left = jnp.concatenate([h, h, m, h, m, l], axis=1)
        right = jnp.concatenate([h, m, h, l, m, h], axis=1)
        term = dot(left, right, NT)
        g = term if g is None else g + term
    out_ref[0:64, :] = g[0:64, 0:128]
    out_ref[64:128, :] = g[0:64, 128:256]
    out_ref[128:192, :] = g[64:128, 128:256]
    out_ref[192:256, :] = g[128:192, 128:256]
    low_lanes = lax.broadcasted_iota(jnp.int32, (64, 128), 1) < 64
    out_ref[256:320, :] = jnp.where(low_lanes, pltpu.roll(g[192:256, 128:256], 64, 1), g[64:128, 0:128])


def gram(columns):
    return pl.pallas_call(
        gram_kernel,
        out_shape=jax.ShapeDtypeStruct((320, 128), F),
        in_specs=[VM],
        out_specs=VM,
        compiler_params=pltpu.CompilerParams(vmem_limit_bytes=LIMIT),
    )(columns)


def lane_of(x, lane):
    index = jnp.full((8, 128, 1), lane, jnp.int32)
    dims = lax.GatherDimensionNumbers(
        offset_dims=(),
        collapsed_slice_dims=(1,),
        start_index_map=(1,),
        operand_batching_dims=(0,),
        start_indices_batching_dims=(0,),
    )
    return lax.gather(x, index, dims, (1, 1), mode=lax.GatherScatterMode.PROMISE_IN_BOUNDS)


def panel_step(rows, off, width):
    n = len(rows)
    lanes = range(width // 128)
    sub = lax.broadcasted_iota(jnp.int32, (8, 128), 0)
    part = [[[r[8 * g:8 * g + 8, 128 * q:128 * q + 128] for q in lanes] for g in range(4)] for r in rows]
    for s in range(4):
        at = off + 8 * s
        cols = [
            [None if g < s else [lane_of(part[b][g][0], at + j) for j in range(8)] for g in range(4)]
            for b in range(n)
        ]
        pivots = [None] * n
        for j in range(8):
            for b in range(n):
                here = cols[b][s]
                pivot = jnp.broadcast_to(here[j][j:j + 1, :], (8, 128))
                inverse = 1.0 / pivot
                pivots[b] = pivot if j == 0 else jnp.where(sub == j, pivot, pivots[b])
                if j == 7 and s == 3:
                    continue
                across = [
                    None if l <= j else jnp.broadcast_to(here[l][j:j + 1, :], (8, 128)) for l in range(8)
                ]
                row = [jnp.broadcast_to(part[b][s][q][j:j + 1, :], (8, 128)) for q in lanes]
                for g in range(s, 4):
                    if g == s and j == 7:
                        continue
                    c = cols[b][g][j] * inverse
                    for l in range(j + 1, 8):
                        cols[b][g][l] = cols[b][g][l] - c * across[l]
                    if g == s:
                        c = jnp.where(sub > j, c, 0.0)
                    part[b][g] = [part[b][g][q] - c * row[q] for q in lanes]
        for b in range(n):
            scale = lax.rsqrt(pivots[b])
            part[b][s] = [v * scale for v in part[b][s]]
    return [jnp.concatenate([jnp.concatenate(v, axis=1) for v in p], axis=0) for p in part]


def products(rows, lanes):
    h, m, l = split3(rows)
    left = jnp.concatenate([h, h, m, h, m, l], axis=0)[:, :lanes]
    return dot(left, jnp.concatenate([h, m, h, l, m, h], axis=0), TN)


def factor(n, work, upper, beside):
    for c0 in (0, 128):
        for k in range(4):
            r0 = c0 + 32 * k
            rows = panel_step([work[b, r0:r0 + 32, c0:256] for b in range(n)], 32 * k, 256 - c0)
            for b in range(n):
                upper[b, r0:r0 + 32, c0:256] = rows[b]
            lo = r0 + 32
            for b in range(n):
                if k < 3:
                    update = products(rows[b], 128)
                    work[b, lo:c0 + 128, c0:256] = work[b, lo:c0 + 128, c0:256] - update[lo - c0:, :]
                elif c0 == 0:
                    update = products(upper[b, 0:128, 128:256], 128)
                    work[b, 128:256, 128:256] = work[b, 128:256, 128:256] - update
            if c0:
                beside(k)


def factor_kernel(scales, base_ref, mine_ref, others_ref, send_ref, turned, nodes, root, slices_ref, work, upper, left, right, sems):
    n = len(scales)
    copies = []

    def copy(src, dst):
        copies.append(pltpu.make_async_copy(src, dst, sems.at[len(copies)]))
        copies[-1].start()

    for b in range(BLOCKS):
        copy(send_ref.at[b // 2, b % 2], turned.at[:, pl.ds(BOX * b, BOX)])
    core = base_ref[0] // BLOCKS % 2
    slices_ref[core] = mine_ref[...]
    slices_ref[1 - core] = others_ref[...]
    ri = lax.broadcasted_iota(jnp.int32, (128, 128), 0)
    ci = lax.broadcasted_iota(jnp.int32, (128, 128), 1)
    eye = jnp.where(ri == ci, 1.0, 0.0)
    below = ri >= ci
    for b in range(n):
        t = jnp.concatenate([slices_ref[r // 4, r % 4, b] for r in range(8)], axis=0) * scales[b]
        work[b, 0:64, 0:128] = t[0:64] + eye[0:64]
        work[b, 0:64, 128:256] = t[64:128]
        work[b, 64:128, 0:128] = t[256:320] + eye[64:128]
        work[b, 64:128, 128:256] = t[128:192]
        work[b, 128:192, 128:256] = t[192:256] + eye[0:64]
        work[b, 192:256, 128:256] = pltpu.roll(t[256:320], 64, 1) + eye[64:128]

    def place(b, half):
        columns = pl.ds(128 * half, 128)
        return nodes.at[0, b, :, columns] if b < LEVELS else root.at[:, columns]

    def beside(k):
        for b in range(n):
            if k == b // 2:
                left[b, 0:128] = jnp.where(below, upper[b, 0:128, 0:128].T, 0.0)
                left[b, 128:256] = upper[b, 0:128, 128:256].T
                copy(left.at[b], place(b, 0))
            if k == 3:
                right[b, 0:128] = jnp.zeros((128, 128), F)
                right[b, 128:256] = jnp.where(below, upper[b, 128:256, 128:256].T, 0.0)
                copy(right.at[b], place(b, 1))

    factor(n, work, upper, beside)
    for c in copies:
        c.wait()


def factors(base, slices, others, send, scales):
    n = len(scales)
    any_place = pl.BlockSpec(memory_space=pl.ANY)
    return pl.pallas_call(
        functools.partial(factor_kernel, scales),
        out_shape=(
            jax.ShapeDtypeStruct((64, BLOCKS * BOX), F),
            jax.ShapeDtypeStruct((1, LEVELS, 256, 256), F),
            jax.ShapeDtypeStruct((256, 256), F),
        ),
        in_specs=[SM, VM, VM, VM],
        out_specs=(any_place,) * 3,
        scratch_shapes=[pltpu.VMEM((2,) + slices.shape, F)] + [pltpu.VMEM((n, 256, 256), F)] * 2
        + [pltpu.VMEM((n, 256, 128), F)] * 2
        + [pltpu.SemaphoreType.DMA((BLOCKS + 2 * n,))],
        compiler_params=pltpu.CompilerParams(vmem_limit_bytes=LIMIT),
    )(base, slices, others, send)


def line_kernel(base_ref, slices, level2, level3, line):
    z = base_ref[0] // (2 * BLOCKS) % 8
    two = z // 2 * 2
    four = z // 4 * 4
    level2[...] = slices[two] + slices[two + 1]
    level3[...] = (slices[four] + slices[four + 1]) + (slices[four + 2] + slices[four + 3])
    low = (slices[0] + slices[1]) + (slices[2] + slices[3])
    high = (slices[4] + slices[5]) + (slices[6] + slices[7])
    total = low + high
    for k in range(8):
        line[k] = total


def line_sums(base, slices):
    one = jax.ShapeDtypeStruct(slices.shape[1:], F)
    return pl.pallas_call(
        line_kernel,
        out_shape=(one, one, jax.ShapeDtypeStruct(slices.shape, F)),
        in_specs=[SM, VM],
        out_specs=(VM, VM, VM),
        compiler_params=pltpu.CompilerParams(vmem_limit_bytes=LIMIT),
    )(base, slices)


def exchange(x, axes):
    return lax.all_to_all(x, axes, 0, 0)


def to_all(x, axes, n):
    return exchange(jnp.broadcast_to(x[None], (n,) + x.shape), axes)


def body(points, probes, near_list, near_count):
    leaf = ("y", "z", "c")
    size = lax.axis_size(leaf)
    rows = points.shape[0]
    packed = jnp.concatenate([probes.T, points.T], axis=0)
    across = [(i, (i + (1 if i % 2 else -1)) % size) for i in range(size)]
    far = lax.ppermute(packed, leaf, across)
    near = lax.ppermute(packed, leaf, [(i, i ^ 1) for i in range(size)])
    base = (lax.axis_index(leaf) * BLOCKS).astype(jnp.int32).reshape(1)
    part, sides, ids, end = own_tiles(base, near_list, near_count, packed)
    send = halo_tiles(ids, end, near, far, sides, part)
    columns = exchange(send, "x")
    pieces = gram(columns).reshape(8, 40, 128)
    level1 = jnp.sum(exchange(pieces, ("c", "x")), axis=0)
    along_z = to_all(level1, "z", 8)
    level2, level3, line = line_sums(base, along_z)
    along_y = exchange(line, "y")
    root = jnp.sum(along_y, axis=0)
    slices = to_all(jnp.stack([level1, level2, level3, root]), "x", 4)
    others = lax.ppermute(slices, "c", [(0, 1), (1, 0)])
    scales = [1.0 / (rows * 2 ** (l + 1)) for l in range(LEVELS)] + [1.0 / (rows * size)]
    turned, node_factors, root_factor = factors(base, slices, others, send, scales)
    return turned.T, node_factors, root_factor


def solution(mesh):
    fine = Mesh(mesh.devices.reshape(8, 8, 2, 4), ("y", "z", "c", "x"))
    leaf = ("y", "z", "c")
    return jax.shard_map(
        body,
        mesh=fine,
        in_specs=(P(leaf, None), P(leaf, "x"), P(leaf, None), P(leaf)),
        out_specs=(P(leaf, "x"), P(leaf, None, None, None), P()),
        check_vma=False,
    )
```

```python
import functools

import jax
import jax.numpy as jnp
from jax import lax
from jax.experimental import pallas as pl
from jax.experimental.pallas import tpu as pltpu
from jax.sharding import Mesh, PartitionSpec as P

LEVELS = 3
BLOCKS = 8
BOX = 256
SLOTS = 16
GROUP = 8
ENTRIES = BLOCKS * SLOTS + 3 * GROUP
BF = jnp.bfloat16
F = jnp.float32
NN = (((1,), (0,)), ((), ()))
NT = (((1,), (1,)), ((), ()))
TN = (((0,), (0,)), ((), ()))
LOG2E_OVER_32 = 1.4426950408889634 / 32.0
LIMIT = 20 << 20
VM = pl.BlockSpec(memory_space=pltpu.VMEM)
SM = pl.BlockSpec(memory_space=pltpu.SMEM)


def dot(a, b, dims):
    return lax.dot_general(a, b, dims, preferred_element_type=F)


def split3(x):
    h = x.astype(BF)
    r = x - h.astype(F)
    m = r.astype(BF)
    return h, m, (r - m.astype(F)).astype(BF)


def squared(box):
    wide = box[64:128].astype(F)
    sq = jnp.sum(wide * wide, axis=0, keepdims=True)
    h = sq.astype(BF).astype(F)
    m = (sq - h).astype(BF).astype(F)
    return h, m, sq - h - m, lax.broadcasted_iota(jnp.int32, (16, BOX), 0)


def extended(head, points):
    return jnp.concatenate([head.astype(BF), jnp.zeros((48, BOX), BF), points], axis=0)


def other_side(box):
    h, m, l, row = squared(box)
    head = jnp.where(row == 0, h, jnp.where(row == 1, m, jnp.where(row == 2, l, jnp.where(row < 6, 1.0, 0.0))))
    return extended(head, box[64:128]).T


def own_side(box):
    h, m, l, row = squared(box)
    head = jnp.where(row < 3, -1.0, jnp.where(row == 3, -h, jnp.where(row == 4, -m, jnp.where(row == 5, -l, 0.0))))
    return extended(head, (box[64:128].astype(F) * 2.0).astype(BF))


def build_lists(base, list_ref, count_ref, own, halo):
    core = (base // BLOCKS) % 2

    def of_box(b, counts):
        def of_slot(s, counts):
            in_own, in_halo = counts
            j = list_ref[b, s] - base
            own[0, in_own] = b
            own[1, in_own] = j
            halo[0, in_halo] = b
            before = (j < 0).astype(jnp.int32)
            halo[1, in_halo] = jnp.where(j < 0, j + BLOCKS, j - BLOCKS) + BLOCKS * (before ^ core)
            inside = jnp.logical_and(j >= 0, j < BLOCKS).astype(jnp.int32)
            return in_own + inside, in_halo + 1 - inside

        return lax.fori_loop(0, count_ref[b], of_slot, counts)

    return lax.fori_loop(0, BLOCKS, of_box, (jnp.int32(GROUP), jnp.int32(GROUP)))


def run_list(end, ids, own, other, probes, parts, total):
    def make(t, k):
        e = t * GROUP + k
        tile = jnp.exp2(dot(other[ids[1, e]], own[ids[0, e]], NN) * LOG2E_OVER_32)
        h = tile.astype(BF)
        parts[k, 0:BOX] = h
        parts[k, BOX:2 * BOX] = (tile - h.astype(F)).astype(BF)

    def use(t, k):
        e = t * GROUP + k
        left = probes[ids[1, e]]
        i = ids[0, e]
        total[i] = total[i] + dot(jnp.concatenate([left, left], axis=1), parts[k], NN)

    def step(t, _):
        for k in range(GROUP):
            use(t - 1, k)
            make(t, k)
        return 0

    last = jnp.maximum((end - 1) // GROUP, 1)
    for k in range(GROUP):
        make(1, k)
    lax.fori_loop(2, last + 1, step, 0)
    for k in range(GROUP):
        use(last, k)


def own_kernel(
    base_ref, list_hbm, count_hbm, own_ref, total, sides, halo_ids, halo_end,
    other, probes, parts, ids, list_ref, count_ref, sems,
):
    copies = [
        pltpu.make_async_copy(list_hbm, list_ref, sems.at[0]),
        pltpu.make_async_copy(count_hbm, count_ref, sems.at[1]),
    ]
    for copy in copies:
        copy.start()
    for b in range(BLOCKS):
        box = own_ref[:, BOX * b:BOX * b + BOX]
        other[b] = other_side(box)
        sides[b] = own_side(box)
        probes[b] = box[0:64]
    other[BLOCKS] = jnp.zeros((BOX, 128), BF)
    probes[BLOCKS] = jnp.zeros((64, BOX), BF)
    total[...] = jnp.zeros_like(total)
    for copy in copies:
        copy.wait()
    end, end_halo = build_lists(base_ref[0], list_ref, count_ref, ids, halo_ids)
    halo_end[0] = end_halo
    for k in range(GROUP):
        for to, null, last in ((ids, BLOCKS, end), (halo_ids, 2 * BLOCKS, end_halo)):
            to[0, last + k] = 0
            to[1, last + k] = null
    run_list(end, ids, sides, other, probes, parts, total)


def halo_kernel(ids, end_ref, near_ref, far_ref, sides, part, send, other, probes, parts, total):
    for q, ref in enumerate((near_ref, far_ref)):
        for b in range(BLOCKS):
            box = ref[:, BOX * b:BOX * b + BOX]
            other[BLOCKS * q + b] = other_side(box)
            probes[BLOCKS * q + b] = box[0:64]
    other[2 * BLOCKS] = jnp.zeros((BOX, 128), BF)
    probes[2 * BLOCKS] = jnp.zeros((64, BOX), BF)
    total[...] = part[...]
    run_list(end_ref[0], ids, sides, other, probes, parts, total)
    for b in range(BLOCKS):
        send[b // 2, b % 2] = total[b]


def list_scratch(boxes):
    return [
        pltpu.VMEM((boxes + 1, BOX, 128), BF),
        pltpu.VMEM((boxes + 1, 64, BOX), BF),
        pltpu.VMEM((GROUP, 2 * BOX, BOX), BF),
    ]


def tiles_cost():
    return pl.CostEstimate(
        flops=64 * 3 * BOX * BOX * 128 * 2, bytes_accessed=4 << 20, transcendentals=64 * BOX * BOX
    )


def own_tiles(base, near_list, near_count, own):
    return pl.pallas_call(
        own_kernel,
        out_shape=(
            jax.ShapeDtypeStruct((BLOCKS, 64, BOX), F),
            jax.ShapeDtypeStruct((BLOCKS, 128, BOX), BF),
            jax.ShapeDtypeStruct((2, ENTRIES), jnp.int32),
            jax.ShapeDtypeStruct((1,), jnp.int32),
        ),
        in_specs=[SM, pl.BlockSpec(memory_space=pltpu.HBM), pl.BlockSpec(memory_space=pltpu.HBM), VM],
        out_specs=(VM, VM, SM, SM),
        scratch_shapes=list_scratch(BLOCKS)
        + [
            pltpu.SMEM((2, ENTRIES), jnp.int32),
            pltpu.SMEM((BLOCKS, SLOTS), jnp.int32),
            pltpu.SMEM((BLOCKS,), jnp.int32),
            pltpu.SemaphoreType.DMA((2,)),
        ],
        compiler_params=pltpu.CompilerParams(vmem_limit_bytes=LIMIT),
        cost_estimate=tiles_cost(),
    )(base, near_list, near_count, own)


def halo_tiles(ids, end, near, far, sides, part):
    return pl.pallas_call(
        halo_kernel,
        out_shape=jax.ShapeDtypeStruct((BLOCKS // 2, 2, 64, BOX), F),
        in_specs=[SM, SM] + [VM] * 4,
        out_specs=VM,
        scratch_shapes=list_scratch(2 * BLOCKS) + [pltpu.VMEM((BLOCKS, 64, BOX), F)],
        compiler_params=pltpu.CompilerParams(vmem_limit_bytes=LIMIT),
        cost_estimate=tiles_cost(),
    )(ids, end, near, far, sides, part)


def gram_kernel(columns_ref, out_ref):
    g = None
    for b in range(2):
        h, m, l = split3(jnp.concatenate([columns_ref[q, b] for q in range(4)], axis=0))
        left = jnp.concatenate([h, h, m, h, m, l], axis=1)
        right = jnp.concatenate([h, m, h, l, m, h], axis=1)
        term = dot(left, right, NT)
        g = term if g is None else g + term
    out_ref[0:64, :] = g[0:64, 0:128]
    out_ref[64:128, :] = g[0:64, 128:256]
    out_ref[128:192, :] = g[64:128, 128:256]
    out_ref[192:256, :] = g[128:192, 128:256]
    low_lanes = lax.broadcasted_iota(jnp.int32, (64, 128), 1) < 64
    out_ref[256:320, :] = jnp.where(low_lanes, pltpu.roll(g[192:256, 128:256], 64, 1), g[64:128, 0:128])


def gram(columns):
    return pl.pallas_call(
        gram_kernel,
        out_shape=jax.ShapeDtypeStruct((320, 128), F),
        in_specs=[VM],
        out_specs=VM,
        compiler_params=pltpu.CompilerParams(vmem_limit_bytes=LIMIT),
    )(columns)


def lane_of(x, lane):
    index = jnp.full((8, 128, 1), lane, jnp.int32)
    dims = lax.GatherDimensionNumbers(
        offset_dims=(),
        collapsed_slice_dims=(1,),
        start_index_map=(1,),
        operand_batching_dims=(0,),
        start_indices_batching_dims=(0,),
    )
    return lax.gather(x, index, dims, (1, 1), mode=lax.GatherScatterMode.PROMISE_IN_BOUNDS)


def panel_step(rows, off, width):
    n = len(rows)
    lanes = range(width // 128)
    sub = lax.broadcasted_iota(jnp.int32, (8, 128), 0)
    part = [[[r[8 * g:8 * g + 8, 128 * q:128 * q + 128] for q in lanes] for g in range(4)] for r in rows]
    for s in range(4):
        at = off + 8 * s
        cols = [
            [None if g < s else [lane_of(part[b][g][0], at + j) for j in range(8)] for g in range(4)]
            for b in range(n)
        ]
        pivots = [None] * n
        for j in range(8):
            for b in range(n):
                here = cols[b][s]
                pivot = jnp.broadcast_to(here[j][j:j + 1, :], (8, 128))
                inverse = 1.0 / pivot
                pivots[b] = pivot if j == 0 else jnp.where(sub == j, pivot, pivots[b])
                if j == 7 and s == 3:
                    continue
                across = [
                    None if l <= j else jnp.broadcast_to(here[l][j:j + 1, :], (8, 128)) for l in range(8)
                ]
                row = [jnp.broadcast_to(part[b][s][q][j:j + 1, :], (8, 128)) for q in lanes]
                for g in range(s, 4):
                    if g == s and j == 7:
                        continue
                    c = cols[b][g][j] * inverse
                    for l in range(j + 1, 8):
                        cols[b][g][l] = cols[b][g][l] - c * across[l]
                    if g == s:
                        c = jnp.where(sub > j, c, 0.0)
                    part[b][g] = [part[b][g][q] - c * row[q] for q in lanes]
        for b in range(n):
            scale = lax.rsqrt(pivots[b])
            part[b][s] = [v * scale for v in part[b][s]]
    return [jnp.concatenate([jnp.concatenate(v, axis=1) for v in p], axis=0) for p in part]


def products(rows, lanes):
    h, m, l = split3(rows)
    left = jnp.concatenate([h, h, m, h, m, l], axis=0)[:, :lanes]
    return dot(left, jnp.concatenate([h, m, h, l, m, h], axis=0), TN)


def factor(n, work, upper, beside):
    for c0 in (0, 128):
        for k in range(4):
            r0 = c0 + 32 * k
            rows = panel_step([work[b, r0:r0 + 32, c0:256] for b in range(n)], 32 * k, 256 - c0)
            for b in range(n):
                upper[b, r0:r0 + 32, c0:256] = rows[b]
            lo = r0 + 32
            for b in range(n):
                if k < 3:
                    update = products(rows[b], 128)
                    work[b, lo:c0 + 128, c0:256] = work[b, lo:c0 + 128, c0:256] - update[lo - c0:, :]
                elif c0 == 0:
                    update = products(upper[b, 0:128, 128:256], 128)
                    work[b, 128:256, 128:256] = work[b, 128:256, 128:256] - update
            if c0:
                beside(k)


def factor_kernel(scales, base_ref, mine_ref, others_ref, send_ref, turned, nodes, root, slices_ref, work, upper, left, right, sems):
    n = len(scales)
    copies = []

    def copy(src, dst):
        copies.append(pltpu.make_async_copy(src, dst, sems.at[len(copies)]))
        copies[-1].start()

    for b in range(BLOCKS):
        copy(send_ref.at[b // 2, b % 2], turned.at[:, pl.ds(BOX * b, BOX)])
    core = base_ref[0] // BLOCKS % 2
    slices_ref[core] = mine_ref[...]
    slices_ref[1 - core] = others_ref[...]
    ri = lax.broadcasted_iota(jnp.int32, (128, 128), 0)
    ci = lax.broadcasted_iota(jnp.int32, (128, 128), 1)
    eye = jnp.where(ri == ci, 1.0, 0.0)
    below = ri >= ci
    for b in range(n):
        t = jnp.concatenate([slices_ref[r // 4, r % 4, b] for r in range(8)], axis=0) * scales[b]
        work[b, 0:64, 0:128] = t[0:64] + eye[0:64]
        work[b, 0:64, 128:256] = t[64:128]
        work[b, 64:128, 0:128] = t[256:320] + eye[64:128]
        work[b, 64:128, 128:256] = t[128:192]
        work[b, 128:192, 128:256] = t[192:256] + eye[0:64]
        work[b, 192:256, 128:256] = pltpu.roll(t[256:320], 64, 1) + eye[64:128]

    def place(b, half):
        columns = pl.ds(128 * half, 128)
        return nodes.at[0, b, :, columns] if b < LEVELS else root.at[:, columns]

    def beside(k):
        for b in range(n):
            if k == b // 2:
                left[b, 0:128] = jnp.where(below, upper[b, 0:128, 0:128].T, 0.0)
                left[b, 128:256] = upper[b, 0:128, 128:256].T
                copy(left.at[b], place(b, 0))
            if k == 3:
                right[b, 0:128] = jnp.zeros((128, 128), F)
                right[b, 128:256] = jnp.where(below, upper[b, 128:256, 128:256].T, 0.0)
                copy(right.at[b], place(b, 1))

    factor(n, work, upper, beside)
    for c in copies:
        c.wait()


def factors(base, slices, others, send, scales):
    n = len(scales)
    any_place = pl.BlockSpec(memory_space=pl.ANY)
    return pl.pallas_call(
        functools.partial(factor_kernel, scales),
        out_shape=(
            jax.ShapeDtypeStruct((64, BLOCKS * BOX), F),
            jax.ShapeDtypeStruct((1, LEVELS, 256, 256), F),
            jax.ShapeDtypeStruct((256, 256), F),
        ),
        in_specs=[SM, VM, VM, VM],
        out_specs=(any_place,) * 3,
        scratch_shapes=[pltpu.VMEM((2,) + slices.shape, F)] + [pltpu.VMEM((n, 256, 256), F)] * 2
        + [pltpu.VMEM((n, 256, 128), F)] * 2
        + [pltpu.SemaphoreType.DMA((BLOCKS + 2 * n,))],
        compiler_params=pltpu.CompilerParams(vmem_limit_bytes=LIMIT),
    )(base, slices, others, send)


def line_kernel(base_ref, slices, level2, level3, line):
    z = base_ref[0] // (2 * BLOCKS) % 8
    two = z // 2 * 2
    four = z // 4 * 4
    level2[...] = slices[two] + slices[two + 1]
    level3[...] = (slices[four] + slices[four + 1]) + (slices[four + 2] + slices[four + 3])
    low = (slices[0] + slices[1]) + (slices[2] + slices[3])
    high = (slices[4] + slices[5]) + (slices[6] + slices[7])
    total = low + high
    for k in range(8):
        line[k] = total


def line_sums(base, slices):
    one = jax.ShapeDtypeStruct(slices.shape[1:], F)
    return pl.pallas_call(
        line_kernel,
        out_shape=(one, one, jax.ShapeDtypeStruct(slices.shape, F)),
        in_specs=[SM, VM],
        out_specs=(VM, VM, VM),
        compiler_params=pltpu.CompilerParams(vmem_limit_bytes=LIMIT),
    )(base, slices)


def sum_of(slices):
    low = (slices[0] + slices[1]) + (slices[2] + slices[3])
    return low + ((slices[4] + slices[5]) + (slices[6] + slices[7]))


def first_kernel(slices, level1, spread):
    total = sum_of(slices)
    level1[...] = total
    for k in range(8):
        spread[k] = total


def last_kernel(slices, level1, level2, level3, spread):
    levels = (level1[...], level2[...], level3[...], sum_of(slices))
    for k in range(4):
        for l, x in enumerate(levels):
            spread[k, l] = x


def first_sums(slices):
    return pl.pallas_call(
        first_kernel,
        out_shape=(jax.ShapeDtypeStruct(slices.shape[1:], F), jax.ShapeDtypeStruct(slices.shape, F)),
        in_specs=[VM],
        out_specs=(VM, VM),
        compiler_params=pltpu.CompilerParams(vmem_limit_bytes=LIMIT),
    )(slices)


def last_sums(slices, level1, level2, level3):
    return pl.pallas_call(
        last_kernel,
        out_shape=jax.ShapeDtypeStruct((4, LEVELS + 1) + slices.shape[1:], F),
        in_specs=[VM] * 4,
        out_specs=VM,
        compiler_params=pltpu.CompilerParams(vmem_limit_bytes=LIMIT),
    )(slices, level1, level2, level3)


def exchange(x, axes):
    return lax.all_to_all(x, axes, 0, 0)


def body(points, probes, near_list, near_count):
    leaf = ("y", "z", "c")
    size = lax.axis_size(leaf)
    rows = points.shape[0]
    packed = jnp.concatenate([probes.T, points.T], axis=0)
    across = [(i, (i + (1 if i % 2 else -1)) % size) for i in range(size)]
    far = lax.ppermute(packed, leaf, across)
    near = lax.ppermute(packed, leaf, [(i, i ^ 1) for i in range(size)])
    base = (lax.axis_index(leaf) * BLOCKS).astype(jnp.int32).reshape(1)
    part, sides, ids, end = own_tiles(base, near_list, near_count, packed)
    send = halo_tiles(ids, end, near, far, sides, part)
    columns = exchange(send, "x")
    pieces = gram(columns).reshape(8, 40, 128)
    level1, spread = first_sums(exchange(pieces, ("c", "x")))
    along_z = exchange(spread, "z")
    level2, level3, line = line_sums(base, along_z)
    along_y = exchange(line, "y")
    slices = exchange(last_sums(along_y, level1, level2, level3), "x")
    others = lax.ppermute(slices, "c", [(0, 1), (1, 0)])
    scales = [1.0 / (rows * 2 ** (l + 1)) for l in range(LEVELS)] + [1.0 / (rows * size)]
    turned, node_factors, root_factor = factors(base, slices, others, send, scales)
    return turned.T, node_factors, root_factor


def solution(mesh):
    fine = Mesh(mesh.devices.reshape(8, 8, 2, 4), ("y", "z", "c", "x"))
    leaf = ("y", "z", "c")
    return jax.shard_map(
        body,
        mesh=fine,
        in_specs=(P(leaf, None), P(leaf, "x"), P(leaf, None), P(leaf)),
        out_specs=(P(leaf, "x"), P(leaf, None, None, None), P()),
        check_vma=False,
    )
```
